512 devices in a mesh: ctx: 64 (over y, x, core), grp: 8 (over z).
Axes of the slice: x: 4, y: 8, z: 8, core: 2. Of those that a mesh axis runs over, the one named last changes fastest.
Arguments:
- x_in: bfloat16 [8192, 16384], P('ctx', 'grp'), may hold values from -0.29882812 to 0.29882812
- b_in: bfloat16 [8192, 128], P('ctx'), may hold values from -6 to 6
- c_in: bfloat16 [8192, 128], P('ctx'), may hold values from -0.52734375 to 0.52734375
- decay_log: float32 [128, 8192], P('grp', 'ctx'), may hold values from -1 to 0
- q_in: bfloat16 [8192, 4096], P('ctx', 'grp'), may hold values from -64 to 64
- k_in: bfloat16 [8192, 1024], P('ctx', 'grp'), may hold values from -4 to 4
- v_in: bfloat16 [8192, 1024], P('ctx', 'grp'), may hold values from -6 to 6
- expert_ids: int32 [8192, 2], P(('ctx', 'grp')), may hold values from 0 to 15, all different within a row; in each aligned block of 16 rows (0 to 15, 16 to 31, ...) at most 4 rows name the same one
- gates: float32 [8192, 2], P(('ctx', 'grp')), may hold values from 0.2 to 1
- expert_out: bfloat16 [64, 16, 8, 4, 8192], P('ctx', 'grp'), may hold values from -6 to 6
Outputs:
- mamba_out: bfloat16 [8192, 16384], P('ctx', 'grp')
- attn_out: bfloat16 [8192, 4096], P('ctx', 'grp')
- moe_out: bfloat16 [8192, 8192], P(('ctx', 'grp'))
The draws below stay inside these ranges and needn't reach their ends.
Inputs may be any that keep to these rules, and one draw needn't show every extreme that they name: `expert_ids`: within the 16 rows of one device no expert is named more than 4 times; each row names 2 different experts.
All inputs are finite; a program needn't handle non-finite values.
Results may differ from the reference program's by a relative error of at most 0.0047.
Values may be sent and summed in bfloat16 or wider, within the bound.
No kernel may reach another device: no remote copies, remote signals or barrier semaphores. Data moves between devices by JAX's collectives and lax.ppermute only.
A program may use at most 192 MiB of HBM per device.

```python
import math
import jax
import jax.numpy as jnp
import numpy as np
from jax import lax

D = 8192
HD = 128
KVHEADS = 8
QHEADS = 32
MHEADS = 128
MP = 128
NST = 128
EXPERTS = 16
TOP = 2
TOK_DEV = 128
PROMPT_TOKENS = 8192
MTOK_DEV = 16
CAP = 4
N_CTX = 64
N_GRP = 8


def drawn_keys(key):
    width_all = KVHEADS * HD
    base_key = jax.random.fold_in(key, 101)
    base = jnp.clip(jax.random.normal(base_key, (PROMPT_TOKENS, width_all), jnp.float32), -4.0, 4.0)
    return base


def draw_k_in(key, part):
    keys_all = drawn_keys(key)
    return keys_all.astype(jnp.bfloat16)


def draw_q_in(key, part):
    own_key = jax.random.fold_in(key, 103)
    row_scale = jnp.exp(jax.random.uniform(jax.random.fold_in(key, 104), (PROMPT_TOKENS, 1), jnp.float32, 0.0, math.log(16.0)))
    base = jnp.clip(jax.random.normal(own_key, (PROMPT_TOKENS, QHEADS * HD), jnp.float32), -4.0, 4.0) * row_scale
    return base.astype(jnp.bfloat16)


def draw_decay_log(key, part):
    key = jax.random.fold_in(key, 5)
    split_random_key = jax.random.split(key, 7)
    slow_share = 0.5
    chooser = jax.random.uniform(split_random_key[0], (MHEADS, 1), jnp.float32)
    slow_rate = jnp.exp(jax.random.uniform(split_random_key[1], (MHEADS, 1), jnp.float32, math.log(0.1), math.log(1.0))) / PROMPT_TOKENS
    quick_rate = jnp.exp(jax.random.uniform(split_random_key[2], (MHEADS, 1), jnp.float32, math.log(1.0 / (4.0 * TOK_DEV)), math.log(1.0 / 40.0)))
    decay_rate = jnp.where(chooser < slow_share, slow_rate, quick_rate)
    coarse_estimate = jax.random.uniform(split_random_key[3], (MHEADS, PROMPT_TOKENS), jnp.float32, 0.5, 1.5)
    spike_position = jax.random.randint(split_random_key[4], (2,), 0, PROMPT_TOKENS)
    token_offsets = jnp.arange(PROMPT_TOKENS, dtype=jnp.int32)
    surge_magnitude = jnp.any(token_offsets[None, :] == spike_position[:, None], axis=0)
    retained_rows = jax.random.uniform(split_random_key[5], (PROMPT_TOKENS,), jnp.float32, 0.5, 0.8)
    trailing_onset = PROMPT_TOKENS - TOK_DEV + jax.random.randint(split_random_key[6], (), TOK_DEV // 2, TOK_DEV - 1)
    trailing_surge = jnp.logical_or(token_offsets == trailing_onset, token_offsets == trailing_onset + 1)
    value_entry = -decay_rate * coarse_estimate + jnp.where(surge_magnitude, jnp.log(retained_rows), 0.0)[None, :]
    return jnp.where(trailing_surge[None, :], -1.0, value_entry)


def levels(rng, shape, shards, least, high):
    gain = 1.0
    for axis_at, shards_of in shards:
        draws = jax.random.uniform(jax.random.fold_in(jax.random.fold_in(rng, 6), axis_at), (shards_of,), jnp.float32, least / len(shards), high / len(shards))
        gain = gain * jnp.repeat(jnp.exp(draws), shape[axis_at] // shards_of).reshape((-1,) + (1,) * (len(shape) - 1 - axis_at))
    return gain


def routed_block(rng, own, number, rows, count, top, most, lean):
    sequence = jax.random.permutation(rng, count)
    crowded, ordinary = portions_of(count, rows * top, most, lean, True), portions_of(count, rows * top, most, lean, False)
    places = jnp.arange(count)

    def named(lengths, rotation):
        used = int((lengths > 0).sum())
        fixed = max(1, used // 4)
        moved = fixed + (places - fixed + rotation * (used - fixed)) % max(1, count - fixed)
        return jnp.zeros((count,), jnp.int32).at[sequence[jnp.where(places < fixed, places, moved)]].set(jnp.asarray(lengths, jnp.int32))

    lengths = jnp.where(number % 4 == 0, named(crowded, number // 4), named(ordinary, number - number // 4 - 1))
    mixed = jax.random.permutation(jax.random.fold_in(own, 3), count)
    donor, receiver = mixed[0:count // 2 * 2:2], mixed[1:count // 2 * 2:2]
    margin = jnp.minimum(lengths[donor] - 1, most - lengths[receiver]) // 2
    margin = jnp.where((donor == sequence[0]) | (receiver == sequence[0]) | (lengths[receiver] == 0), 0, jnp.maximum(margin, 0))
    moved = jax.random.randint(jax.random.fold_in(own, 4), (count // 2,), 0, 1 << 20) % (margin + 1)
    lengths = lengths.at[donor].add(-moved).at[receiver].add(moved)
    members = jnp.searchsorted(jnp.cumsum(lengths), jnp.arange(rows * top), side="right").astype(jnp.int32)
    grid = members.reshape(top, rows).T
    grid = grid[jax.random.permutation(jax.random.fold_in(own, 1), rows)]
    rotation = jax.random.randint(jax.random.fold_in(own, 2), (rows, 1), 0, top)
    return jnp.take_along_axis(grid, (jnp.arange(top)[None, :] + rotation) % top, axis=1)


def portions_of(count, total, bound, lean, full):
    loads = [(1 << 20) // math.isqrt(grade ** lean) + 1 for grade in range(1, count + 1)]
    largest = bound if full else min(bound, max(-(-total // count), total * loads[0] // sum(loads)))
    least = 1 if total - largest >= count - 1 else 0
    holding, surplus = [largest] + [least] * (count - 1), total - largest - least * (count - 1)
    while surplus > 0:
        candidates = [i for i in range(1, count) if holding[i] < largest] or [i for i in range(1, count) if holding[i] < bound]
        pool, budget = sum([loads[i] for i in candidates]), surplus
        for i in candidates:
            addition = min(bound - holding[i], max(1, budget * loads[i] // pool), surplus)
            holding[i] = holding[i] + addition
            surplus = surplus - addition
    return np.array(holding)


def noise(key, dims, width, reach, pieces=(), held_as=jnp.bfloat16):
    array = jax.random.normal(key, dims, jnp.float32) * width
    if len(pieces) > 0:
        array = levels(key, dims, pieces, -0.22, 0.18) * array
    return jnp.clip(array, min=-reach, max=reach).astype(held_as)


def setup_inputs(seed: int = 0) -> dict:
    key_list = jax.random.split(jax.random.key(seed), 11)
    x_in = noise(key_list[0], (PROMPT_TOKENS, MHEADS * MP), 0.05, 0.29882812, ((0, 64), (1, 8)))
    b_in = noise(key_list[1], (PROMPT_TOKENS, NST), 1.0, 6.0, ((0, 64),))
    c_in = noise(key_list[2], (PROMPT_TOKENS, NST), 0.088, 0.52734375, ((0, 64),))
    decay_log = draw_decay_log(jax.random.fold_in(key_list[10], 71), 0)
    q_in = draw_q_in(jax.random.fold_in(key_list[10], 71), 0)
    k_in = draw_k_in(jax.random.fold_in(key_list[10], 71), 0)
    v_in = noise(key_list[6], (PROMPT_TOKENS, KVHEADS * HD), 1.0, 6.0, ((0, 64), (1, 8)))
    expert_ids_keys = jax.random.split(jax.random.fold_in(key_list[7], 1), PROMPT_TOKENS // MTOK_DEV)
    expert_ids_turns = jax.random.permutation(jax.random.fold_in(key_list[7], 3), PROMPT_TOKENS // MTOK_DEV)
    expert_ids = jax.vmap(lambda own, number: routed_block(jax.random.fold_in(key_list[7], 2), own, number, MTOK_DEV, EXPERTS, TOP, CAP, 2))(expert_ids_keys, expert_ids_turns).reshape((PROMPT_TOKENS, TOP))
    gates = jnp.clip(0.2 + 0.8 * jax.random.uniform(key_list[8], (PROMPT_TOKENS, TOP), jnp.float32) ** levels(key_list[8], (PROMPT_TOKENS, TOP), ((0, 512),), -0.2, 0.2), 0.2, 1.0)
    expert_out = noise(key_list[9], (N_CTX, EXPERTS, N_GRP, CAP, D), 1.0, 6.0, ((0, 64), (1, 8)))
    return dict(x_in=x_in, b_in=b_in, c_in=c_in, decay_log=decay_log, q_in=q_in, k_in=k_in, v_in=v_in, expert_ids=expert_ids, gates=gates, expert_out=expert_out)


def mamba_block(entering, block):
    x_block, b_block, c_block, decay_block = block
    cumulative = jnp.cumsum(decay_block, axis=1)
    cross_block = jnp.dot(c_block, b_block.T, preferred_element_type=jnp.float32)
    length = cumulative.shape[1]
    token_offsets = jnp.arange(length, dtype=jnp.int32)
    causal_mask = token_offsets[:, None] >= token_offsets[None, :]
    log_gap = jnp.where(causal_mask[None], cumulative[:, :, None] - cumulative[:, None, :], -jnp.inf)
    blended_weights = (jnp.exp(log_gap) * cross_block[None]).astype(jnp.bfloat16)
    local_part = jnp.einsum('hts,shp->thp', blended_weights.astype(jnp.float32), x_block.astype(jnp.float32), precision=lax.Precision.HIGHEST)
    tail_decay = jnp.exp(cumulative[:, -1:] - cumulative)
    weighted_b = (tail_decay[:, :, None] * b_block.astype(jnp.float32)[None]).astype(jnp.bfloat16)
    block_state = jnp.einsum('shp,hsn->hpn', x_block.astype(jnp.float32), weighted_b.astype(jnp.float32), precision=lax.Precision.HIGHEST)
    readout = jnp.einsum('tn,hpn->thp', c_block.astype(jnp.float32), entering, precision=lax.Precision.HIGHEST)
    carried_part = jnp.exp(cumulative).T[:, :, None] * readout
    output = (local_part + carried_part).astype(jnp.bfloat16)
    block_decay = jnp.exp(cumulative[:, -1])
    return (block_decay[:, None, None] * entering + block_state, output)

def mamba_layer(x_in, b_in, c_in, decay_log):
    tokens = x_in.shape[0]
    head_count = decay_log.shape[0]
    head_width = x_in.shape[1] // head_count
    state_tensors = b_in.shape[1]
    blocks = tokens // TOK_DEV
    x_blocks = x_in.reshape(blocks, TOK_DEV, head_count, head_width)
    b_blocks = b_in.reshape(blocks, TOK_DEV, state_tensors)
    c_blocks = c_in.reshape(blocks, TOK_DEV, state_tensors)
    decay_blocks = decay_log.reshape(head_count, blocks, TOK_DEV).transpose(1, 0, 2)
    start_state = jnp.zeros((head_count, head_width, state_tensors), jnp.float32)
    final_state, outputs = lax.scan(mamba_block, start_state, (x_blocks, b_blocks, c_blocks, decay_blocks))
    return outputs.reshape(tokens, head_count * head_width)

def attention_layer(q_in, k_in, v_in):
    tokens = q_in.shape[0]
    q_count = q_in.shape[1] // HD
    kv_count = k_in.shape[1] // HD
    group_size = q_count // kv_count
    query_heads = q_in.reshape(tokens, q_count, HD).transpose(1, 0, 2)
    key_heads = k_in.reshape(tokens, kv_count, HD).transpose(1, 0, 2)
    value_heads = v_in.reshape(tokens, kv_count, HD).transpose(1, 0, 2)
    query_block = math.gcd(tokens, 512)
    query_blocks = tokens // query_block
    scale = 1.0 / math.sqrt(HD)
    key_positions = jnp.arange(tokens, dtype=jnp.int32)

    def one_block(index):
        head = index // query_blocks
        which_block = index % query_blocks
        kv_head = head // group_size
        query_rows = lax.dynamic_slice_in_dim(lax.dynamic_index_in_dim(query_heads, head, 0, False), which_block * query_block, query_block, 0)
        keys = lax.dynamic_index_in_dim(key_heads, kv_head, 0, False)
        values = lax.dynamic_index_in_dim(value_heads, kv_head, 0, False)
        scores = jnp.dot(query_rows, keys.T, preferred_element_type=jnp.float32) * scale
        query_positions = which_block * query_block + jnp.arange(query_block, dtype=jnp.int32)
        allowed = key_positions[None, :] <= query_positions[:, None]
        scores = jnp.where(allowed, scores, -jnp.inf)
        largest = lax.optimization_barrier(jnp.max(scores, axis=1, keepdims=True))
        probs = jnp.exp(scores - largest)
        total = lax.optimization_barrier(jnp.sum(probs, axis=1, keepdims=True))
        summed = jnp.dot(probs.astype(jnp.bfloat16), values, preferred_element_type=jnp.float32)
        return (summed / total).astype(jnp.bfloat16)
    results = lax.map(one_block, jnp.arange(q_count * query_blocks, dtype=jnp.int32))
    results = results.reshape(q_count, tokens, HD).transpose(1, 0, 2)
    return results.reshape(tokens, q_count * HD)

def expert_layer(expert_ids, gates, expert_out):
    ctx_count, expert_count, grp_count, capacity, model_width = expert_out.shape
    tokens, top_count = expert_ids.shape
    group_count = ctx_count * grp_count
    per_group = tokens // group_count
    flattened_identifiers = expert_ids.reshape(group_count, per_group * top_count)
    onehot = (flattened_identifiers[:, :, None] == jnp.arange(expert_count, dtype=jnp.int32)[None, None, :]).astype(jnp.int32)
    before = jnp.cumsum(onehot, axis=1, dtype=jnp.int32) - onehot
    slot_index = lax.optimization_barrier(jnp.sum(before * onehot, axis=2, dtype=jnp.int32)).reshape(tokens, top_count)
    group_of = jnp.arange(tokens, dtype=jnp.int32) // per_group
    ctx_of = group_of // grp_count
    source_of = group_of % grp_count
    row_table = expert_out.reshape(ctx_count * expert_count * grp_count * capacity, model_width)
    combined = jnp.zeros((tokens, model_width), jnp.float32)
    for which_one in range(top_count):
        row_number = ((ctx_of * expert_count + expert_ids[:, which_one]) * grp_count + source_of) * capacity + slot_index[:, which_one]
        combined = combined + gates[:, which_one:which_one + 1] * row_table[row_number.astype(jnp.int32)].astype(jnp.float32)
    return combined.astype(jnp.bfloat16)

def reference(x_in, b_in, c_in, decay_log, q_in, k_in, v_in, expert_ids, gates, expert_out):
    mamba_out = mamba_layer(x_in, b_in, c_in, decay_log)
    attn_out = attention_layer(q_in, k_in, v_in)
    moe_out = expert_layer(expert_ids, gates, expert_out)
    return (mamba_out, attn_out, moe_out)
```

```python
import math

import jax
import jax.numpy as jnp
from jax import lax
from jax.experimental import pallas as pl
from jax.experimental.pallas import tpu as pltpu
from jax.sharding import PartitionSpec as P

HD = 128
L = 128
MH = 16
NCTX = 64
QH = 4
CAP = 4
LOG2E = 1.4426950408889634
F32 = jnp.float32
BF16 = jnp.bfloat16
VM = pl.BlockSpec(memory_space=pltpu.VMEM)
SM = pl.BlockSpec(memory_space=pltpu.SMEM)


def params(mib=40):
    return pltpu.CompilerParams(vmem_limit_bytes=mib * 2**20)


def cost(flops, nbytes):
    return pl.CostEstimate(flops=flops, bytes_accessed=nbytes, transcendentals=0)


def tri(lower):
    r = lax.broadcasted_iota(jnp.int32, (L, L), 0)
    c = lax.broadcasted_iota(jnp.int32, (L, L), 1)
    return (c <= r) if lower else (r <= c)


def row_cumulative(decay):
    return jnp.dot(
        decay, tri(False).astype(F32), precision=lax.Precision.HIGHEST, preferred_element_type=F32
    )


def col_cumulative(decay):
    return lax.dot_general(
        tri(True).astype(F32),
        decay,
        (((1,), (1,)), ((), ())),
        precision=lax.Precision.HIGHEST,
        preferred_element_type=F32,
    )


def pack_kernel(k_ref, v_ref, o_ref):
    o_ref[0:HD, :] = k_ref[...].astype(F32).T.astype(BF16)
    o_ref[HD:, :] = v_ref[...]


def pack_kv(k_in, v_in):
    return pl.pallas_call(
        pack_kernel,
        out_shape=jax.ShapeDtypeStruct((2 * HD, L), BF16),
        in_specs=[VM, VM],
        out_specs=VM,
        compiler_params=params(),
        cost_estimate=cost(1 << 20, 1 << 17),
    )(k_in, v_in)


def state_kernel(x_ref, b_ref, d_ref, o_ref):
    cum = row_cumulative(d_ref[...])
    tail = jnp.exp(cum[:, L - 1 :] - cum)
    block_decay = jnp.exp(cum[:, L - 1 :])
    bt = b_ref[...].astype(F32).T
    row = lax.broadcasted_iota(jnp.int32, (8, L), 0)
    for h in range(MH):
        wb = (tail[h : h + 1, :] * bt).astype(BF16)
        s = jnp.dot(wb, x_ref[:, h * HD : (h + 1) * HD], preferred_element_type=F32)
        d = jnp.broadcast_to(block_decay[h : h + 1, :], (8, L))
        hi = d.astype(BF16).astype(F32)
        mid = (d - hi).astype(BF16).astype(F32)
        lo = d - hi - mid
        terms = jnp.where(row == 0, hi, jnp.where(row == 1, mid, jnp.where(row == 2, lo, 0.0)))
        for q in range(4):
            o_ref[h * 4 + q] = jnp.concatenate([s[q * 32 : (q + 1) * 32], terms], axis=0).astype(BF16)


def block_states(x_in, b_in, decay_log):
    return pl.pallas_call(
        state_kernel,
        out_shape=jax.ShapeDtypeStruct((NCTX, 40, HD), BF16),
        in_specs=[VM] * 3,
        out_specs=VM,
        compiler_params=params(),
        cost_estimate=cost(1 << 26, 1 << 20),
    )(x_in, b_in, decay_log)


def scan_kernel(s_ref, o_ref):
    def step(k, e):
        o_ref[k] = e.astype(BF16)
        block = s_ref[k].astype(F32)
        d = block[32:33] + block[33:34] + block[34:35]
        return d * e + block[:32]

    lax.fori_loop(0, NCTX, step, jnp.zeros((32, HD), F32), unroll=8)


def scan_states(pieces):
    return pl.pallas_call(
        scan_kernel,
        out_shape=jax.ShapeDtypeStruct((NCTX, 32, HD), BF16),
        in_specs=[VM],
        out_specs=VM,
        compiler_params=params(),
        cost_estimate=cost(1 << 20, 1 << 20),
    )(pieces)


def local_kernel(x_ref, b_ref, c_ref, d_ref, o_ref):
    cum = row_cumulative(d_ref[...])
    cum_col = col_cumulative(d_ref[...])
    cross = lax.dot_general(
        c_ref[...], b_ref[...], (((1,), (1,)), ((), ())), preferred_element_type=F32
    )
    mask = tri(True)
    for h in range(MH):
        gap = jnp.where(mask, cum_col[:, h : h + 1] - cum[h : h + 1, :], -1e30)
        w = (jnp.exp(gap) * cross).astype(BF16)
        o_ref[:, h * HD : (h + 1) * HD] = jnp.dot(
            w, x_ref[:, h * HD : (h + 1) * HD], preferred_element_type=F32
        )


def local_part(x_in, b_in, c_in, decay_log):
    return pl.pallas_call(
        local_kernel,
        out_shape=jax.ShapeDtypeStruct((L, MH * HD), F32),
        in_specs=[VM] * 4,
        out_specs=VM,
        compiler_params=params(),
        cost_estimate=cost(1 << 28, 1 << 21),
    )(x_in, b_in, c_in, decay_log)


def join_kernel(l_ref, e_ref, c_ref, d_ref, o_ref):
    grow = jnp.exp(col_cumulative(d_ref[...]))
    c = c_ref[...]
    for h in range(MH):
        cols = slice(h * HD, (h + 1) * HD)
        readout = jnp.dot(c, e_ref[cols, :], preferred_element_type=F32)
        o_ref[:, cols] = (l_ref[:, cols] + grow[:, h : h + 1] * readout).astype(BF16)


def join_mamba(local, entering, c_in, decay_log):
    return pl.pallas_call(
        join_kernel,
        out_shape=jax.ShapeDtypeStruct((L, MH * HD), BF16),
        in_specs=[VM] * 4,
        out_specs=VM,
        compiler_params=params(),
        cost_estimate=cost(1 << 26, 1 << 21),
    )(local, entering, c_in, decay_log)


def mamba_part(x_in, b_in, c_in, decay_log):
    pieces = block_states(x_in, b_in, decay_log)
    pieces = lax.all_to_all(pieces, "ctx", split_axis=0, concat_axis=0, tiled=True)
    entering = scan_states(pieces)
    entering = lax.all_to_all(entering, "ctx", split_axis=0, concat_axis=0, tiled=True)
    local = local_part(x_in, b_in, c_in, decay_log)
    return join_mamba(local, entering.reshape(MH * L, HD), c_in, decay_log)


PER = 8


def attention_kernel(me_ref, q_ref, kv_ref, o_ref, m_ref, l_ref, acc_ref):
    step = pl.program_id(0)
    me = me_ref[0]
    c = LOG2E / math.sqrt(HD)
    rows = QH * L

    @pl.when(step == 0)
    def _():
        m_ref[...] = jnp.full((rows, 1), -1e30, F32)
        l_ref[...] = jnp.zeros((rows, L), F32)
        acc_ref[...] = jnp.zeros((rows, HD), F32)

    def work(masked):
        q = jnp.concatenate([q_ref[:, g * HD : (g + 1) * HD] for g in range(QH)], axis=0)
        kt = jnp.concatenate([kv_ref[j, :HD, :] for j in range(PER)], axis=1)
        s = jnp.dot(q, kt, preferred_element_type=F32)
        if masked:
            t = lax.broadcasted_iota(jnp.int32, s.shape, 0) % L
            k = lax.broadcasted_iota(jnp.int32, s.shape, 1)
            s = jnp.where(k <= t + (me - step * PER) * L, s, -1e30)
        m_old = m_ref[...]
        m_new = jnp.maximum(m_old, jnp.max(s, axis=1, keepdims=True))
        factor = jnp.exp2((m_old - m_new) * c)
        p = jnp.exp2((s - m_new) * c)
        total = p[:, :L]
        for j in range(1, PER):
            total = total + p[:, j * L : (j + 1) * L]
        v = jnp.concatenate([kv_ref[j, HD:, :] for j in range(PER)], axis=0)
        added = jnp.dot(p.astype(BF16), v, preferred_element_type=F32)
        m_ref[...] = m_new
        l_ref[...] = l_ref[...] * factor + total
        acc_ref[...] = acc_ref[...] * factor + added

    @pl.when((step + 1) * PER <= me)
    def _():
        work(False)

    @pl.when(jnp.logical_and((step + 1) * PER > me, step * PER <= me))
    def _():
        work(True)

    @pl.when(step == NCTX // PER - 1)
    def _():
        out = acc_ref[...] / jnp.sum(l_ref[...], axis=1, keepdims=True)
        for g in range(QH):
            o_ref[:, g * HD : (g + 1) * HD] = out[g * L : (g + 1) * L].astype(BF16)


def attention_part(q_in, k_in, v_in):
    packed = pack_kv(k_in, v_in)
    gathered = lax.all_gather(packed, "ctx", axis=0, tiled=False)
    me = lax.axis_index("ctx").astype(jnp.int32).reshape(1)
    rows = QH * L
    return pl.pallas_call(
        attention_kernel,
        grid=(NCTX // PER,),
        out_shape=jax.ShapeDtypeStruct((L, QH * HD), BF16),
        in_specs=[
            SM,
            pl.BlockSpec((L, QH * HD), lambda i: (0, 0)),
            pl.BlockSpec((PER, 2 * HD, L), lambda i: (i, 0, 0)),
        ],
        out_specs=pl.BlockSpec((L, QH * HD), lambda i: (0, 0)),
        scratch_shapes=[
            pltpu.VMEM((rows, 1), F32),
            pltpu.VMEM((rows, L), F32),
            pltpu.VMEM((rows, HD), F32),
        ],
        compiler_params=params(),
        cost_estimate=cost(1 << 31, 1 << 22),
    )(me, q_in, gathered)


def combine_kernel(ids_ref, idst_ref, gates_ref, rows_ref, o_ref):
    count = ids_ref.shape[0]
    ids, idst, gates = ids_ref[...], idst_ref[...], gates_ref[...]
    t = lax.broadcasted_iota(jnp.int32, (count, count), 0)
    u = lax.broadcasted_iota(jnp.int32, (count, count), 1)
    place = lax.broadcasted_iota(jnp.int32, (count, rows_ref.shape[0]), 1)
    out = None
    for k in range(2):
        mine = ids[:, k : k + 1]
        slot = jnp.zeros((count, 1), jnp.int32)
        for j in range(2):
            before = (u < t) if j >= k else (u <= t)
            same = jnp.logical_and(before, idst[j : j + 1, :] == mine)
            slot = slot + jnp.sum(same.astype(jnp.int32), axis=1, keepdims=True)
        pick = (place == mine * CAP + slot).astype(F32).astype(BF16)
        row = jnp.dot(pick, rows_ref[...], preferred_element_type=F32)
        term = gates[:, k : k + 1] * row
        out = term if out is None else out + term
    o_ref[...] = out.astype(BF16)


def expert_part(expert_ids, gates, expert_out):
    owned, peers, cap, width = expert_out.shape[1:]
    held = expert_out[0].transpose(1, 0, 2, 3).reshape(peers, owned * cap, width)
    rows = lax.all_to_all(held, "grp", split_axis=0, concat_axis=0, tiled=True)
    rows = rows.reshape(peers * owned * cap, width)
    count = expert_ids.shape[0]
    block = 2048
    return pl.pallas_call(
        combine_kernel,
        grid=(width // block,),
        out_shape=jax.ShapeDtypeStruct((count, width), BF16),
        in_specs=[
            pl.BlockSpec((count, 2), lambda i: (0, 0)),
            pl.BlockSpec((2, count), lambda i: (0, 0)),
            pl.BlockSpec((count, 2), lambda i: (0, 0)),
            pl.BlockSpec((peers * owned * cap, block), lambda i: (0, i)),
        ],
        out_specs=pl.BlockSpec((count, block), lambda i: (0, i)),
        compiler_params=params(),
        cost_estimate=cost(1 << 24, 1 << 20),
    )(expert_ids, expert_ids.T, gates, rows)


def shards(x_in, b_in, c_in, decay_log, q_in, k_in, v_in, expert_ids, gates, expert_out):
    attn_out = attention_part(q_in, k_in, v_in)
    mamba_out = mamba_part(x_in, b_in, c_in, decay_log)
    moe_out = expert_part(expert_ids, gates, expert_out)
    return (mamba_out, attn_out, moe_out)


def solution(mesh):
    return jax.shard_map(
        shards,
        mesh=mesh,
        in_specs=(
            P("ctx", "grp"),
            P("ctx", None),
            P("ctx", None),
            P("grp", "ctx"),
            P("ctx", "grp"),
            P("ctx", "grp"),
            P("ctx", "grp"),
            P(("ctx", "grp"), None),
            P(("ctx", "grp"), None),
            P("ctx", "grp", None, None, None),
        ),
        out_specs=(P("ctx", "grp"), P("ctx", "grp"), P(("ctx", "grp"), None)),
        check_vma=False,
    )
```

```python
import math

import jax
import jax.numpy as jnp
from jax import lax
from jax.experimental import pallas as pl
from jax.experimental.pallas import tpu as pltpu
from jax.sharding import PartitionSpec as P

HD = 128
L = 128
MH = 16
NCTX = 64
QH = 4
CAP = 4
LOG2E = 1.4426950408889634
F32 = jnp.float32
BF16 = jnp.bfloat16
VM = pl.BlockSpec(memory_space=pltpu.VMEM)
SM = pl.BlockSpec(memory_space=pltpu.SMEM)
ANY = pl.BlockSpec(memory_space=pl.ANY)


def params(mib=40):
    return pltpu.CompilerParams(vmem_limit_bytes=mib * 2**20)


def cost(flops, nbytes):
    return pl.CostEstimate(flops=flops, bytes_accessed=nbytes, transcendentals=0)


def tri(lower):
    r = lax.broadcasted_iota(jnp.int32, (L, L), 0)
    c = lax.broadcasted_iota(jnp.int32, (L, L), 1)
    return (c <= r) if lower else (r <= c)


def row_cumulative(decay):
    return jnp.dot(
        decay, tri(False).astype(F32), precision=lax.Precision.HIGHEST, preferred_element_type=F32
    )


def col_cumulative(decay):
    return lax.dot_general(
        tri(True).astype(F32),
        decay,
        (((1,), (1,)), ((), ())),
        precision=lax.Precision.HIGHEST,
        preferred_element_type=F32,
    )


PIECE = 16
KV = 2 * PIECE
SL = 32
CHUNK = KV + SL + 8


def send_kernel(x_ref, b_ref, d_ref, k_ref, v_ref, o_ref):
    cum = row_cumulative(d_ref[...])
    tail = jnp.exp(cum[:, L - 1 :] - cum)
    block_decay = jnp.exp(cum[:, L - 1 :])
    bt = b_ref[...].astype(F32).T
    row = lax.broadcasted_iota(jnp.int32, (8, L), 0)
    pieces = L // PIECE
    for h in range(MH):
        wb = (tail[h : h + 1, :] * bt).astype(BF16)
        s = jnp.dot(wb, x_ref[:, h * HD : (h + 1) * HD], preferred_element_type=F32)
        d = jnp.broadcast_to(block_decay[h : h + 1, :], (8, L))
        hi = d.astype(BF16).astype(F32)
        mid = (d - hi).astype(BF16).astype(F32)
        lo = d - hi - mid
        terms = jnp.where(row == 0, hi, jnp.where(row == 1, mid, jnp.where(row == 2, lo, 0.0)))
        for q in range(4):
            j = h * 4 + q
            rows = slice((j % pieces) * PIECE, (j % pieces + 1) * PIECE)
            o_ref[j, 0:PIECE, :] = k_ref[rows, :]
            o_ref[j, PIECE:KV, :] = v_ref[rows, :]
            o_ref[j, KV:CHUNK, :] = jnp.concatenate(
                [s[q * SL : (q + 1) * SL], terms], axis=0
            ).astype(BF16)


def chunks_to_send(x_in, b_in, decay_log, k_in, v_in):
    return pl.pallas_call(
        send_kernel,
        out_shape=jax.ShapeDtypeStruct((NCTX, CHUNK, HD), BF16),
        in_specs=[VM] * 5,
        out_specs=VM,
        compiler_params=params(),
        cost_estimate=cost(1 << 26, 1 << 21),
    )(x_in, b_in, decay_log, k_in, v_in)


def take_kernel(s_ref, *refs):
    own_ref, o_ref = refs[-2:]
    own_ref[...] = s_ref[:, :KV, :]

    def step(k, e):
        o_ref[k] = e.astype(BF16)
        block = s_ref[k, KV:CHUNK, :].astype(F32)
        d = block[SL : SL + 1] + block[SL + 1 : SL + 2] + block[SL + 2 : SL + 3]
        return d * e + block[:SL]

    lax.fori_loop(0, NCTX, step, jnp.zeros((SL, HD), F32), unroll=8)


def take_received(received, after):
    return pl.pallas_call(
        take_kernel,
        out_shape=[
            jax.ShapeDtypeStruct((NCTX, KV, HD), BF16),
            jax.ShapeDtypeStruct((NCTX, SL, HD), BF16),
        ],
        in_specs=[VM] + [ANY] * len(after),
        out_specs=[VM, VM],
        compiler_params=params(),
        cost_estimate=cost(1 << 20, 1 << 21),
    )(received, *after)


def local_kernel(x_ref, b_ref, c_ref, d_ref, o_ref):
    cum = row_cumulative(d_ref[...])
    cum_col = col_cumulative(d_ref[...])
    cross = lax.dot_general(
        c_ref[...], b_ref[...], (((1,), (1,)), ((), ())), preferred_element_type=F32
    )
    mask = tri(True)
    for h in range(MH):
        gap = jnp.where(mask, cum_col[:, h : h + 1] - cum[h : h + 1, :], -1e30)
        w = (jnp.exp(gap) * cross).astype(BF16)
        o_ref[:, h * HD : (h + 1) * HD] = jnp.dot(
            w, x_ref[:, h * HD : (h + 1) * HD], preferred_element_type=F32
        )


def local_part(x_in, b_in, c_in, decay_log):
    return pl.pallas_call(
        local_kernel,
        out_shape=jax.ShapeDtypeStruct((L, MH * HD), F32),
        in_specs=[VM] * 4,
        out_specs=VM,
        compiler_params=params(),
        cost_estimate=cost(1 << 28, 1 << 21),
    )(x_in, b_in, c_in, decay_log)


def join_kernel(l_ref, e_ref, c_ref, d_ref, o_ref):
    grow = jnp.exp(col_cumulative(d_ref[...]))
    c = c_ref[...]
    for h in range(MH):
        cols = slice(h * HD, (h + 1) * HD)
        readout = jnp.dot(c, e_ref[cols, :], preferred_element_type=F32)
        o_ref[:, cols] = (l_ref[:, cols] + grow[:, h : h + 1] * readout).astype(BF16)


def join_mamba(local, entering, c_in, decay_log):
    return pl.pallas_call(
        join_kernel,
        out_shape=jax.ShapeDtypeStruct((L, MH * HD), BF16),
        in_specs=[VM] * 4,
        out_specs=VM,
        compiler_params=params(),
        cost_estimate=cost(1 << 26, 1 << 21),
    )(local, entering, c_in, decay_log)


ROWS = QH * L
SCALE2 = LOG2E / math.sqrt(HD)


def stacked_queries(q_ref):
    return jnp.concatenate([q_ref[:, g * HD : (g + 1) * HD] for g in range(QH)], axis=0)


def accumulate(state, s, v):
    m_old, total, acc = state
    m = jnp.maximum(m_old, jnp.max(s, axis=1, keepdims=True))
    factor = jnp.exp2((m_old - m) * SCALE2)
    p = jnp.exp2((s - m) * SCALE2)
    part = p[:, :L]
    for j in range(1, p.shape[1] // L):
        part = part + p[:, j * L : (j + 1) * L]
    added = jnp.dot(p.astype(BF16), v, preferred_element_type=F32)
    return m, total * factor + part, acc * factor + added


def scores(q, k):
    return lax.dot_general(q, k, (((1,), (1,)), ((), ())), preferred_element_type=F32)


def attend_kernel(n_sets, first, last, me_ref, q_ref, *refs):
    refs = list(refs)
    if first:
        k_ref, v_ref = refs[:2]
        refs = refs[2:]
    else:
        m_in, l_in, a_in = refs[:3]
        refs = refs[3:]
    sets, refs = refs[:n_sets], refs[n_sets:]
    if last:
        o_ref = refs[0]
        m_ref, l_ref, a_ref = refs[1:]
    else:
        m_ref, l_ref, a_ref = refs
    me = me_ref[0]
    q = stacked_queries(q_ref)
    if first:
        s = scores(q, k_ref[...])
        t = lax.broadcasted_iota(jnp.int32, s.shape, 0) % L
        u = lax.broadcasted_iota(jnp.int32, s.shape, 1)
        s = jnp.where(u <= t, s, -1e30)
        m = jnp.max(s, axis=1, keepdims=True)
        p = jnp.exp2((s - m) * SCALE2)
        m_ref[...] = jnp.broadcast_to(m, (ROWS, L))
        l_ref[...] = p
        a_ref[...] = jnp.dot(p.astype(BF16), v_ref[...], preferred_element_type=F32)
    else:
        m_ref[...] = m_in[...]
        l_ref[...] = l_in[...]
        a_ref[...] = a_in[...]
    shards_in = KEYS // PIECE
    for ref in sets:
        for at in range(ref.shape[0] // shards_in):
            half = at % (NCTX // shards_in)

            def work(ref=ref, at=at, half=half):
                pick = slice(at * shards_in, (at + 1) * shards_in)
                k = ref[pick, 0:PIECE, :].reshape(KEYS, HD)
                v = ref[pick, PIECE:KV, :].reshape(KEYS, HD)
                s = scores(q, k)
                shard = half * shards_in + lax.broadcasted_iota(jnp.int32, (1, KEYS), 1) // PIECE
                s = s + jnp.where(shard < me, 0.0, -1e30)
                m, total, acc = accumulate((m_ref[:, :1], l_ref[...], a_ref[...]), s, v)
                m_ref[...] = jnp.broadcast_to(m, (ROWS, L))
                l_ref[...] = total
                a_ref[...] = acc

            pl.when(half * shards_in < me)(work)
    if last:
        out = a_ref[...] / jnp.sum(l_ref[...], axis=1, keepdims=True)
        for g in range(QH):
            o_ref[:, g * HD : (g + 1) * HD] = out[g * L : (g + 1) * L].astype(BF16)


KEYS = 512


def attend(me, q_in, before, sets, last=False):
    carry = [jax.ShapeDtypeStruct((ROWS, L), F32)] * 3
    first = len(before) == 2

    def kernel(*refs):
        attend_kernel(len(sets), first, last, *refs)

    return pl.pallas_call(
        kernel,
        out_shape=jax.ShapeDtypeStruct((L, QH * HD), BF16) if last else carry,
        in_specs=[SM] + [VM] * (1 + len(before) + len(sets)),
        out_specs=VM if last else [VM] * 3,
        scratch_shapes=[pltpu.VMEM((ROWS, L), F32)] * 3 if last else [],
        compiler_params=params(),
        cost_estimate=cost(1 << 28, len(sets) << 22),
    )(me, q_in, *before, *sets)


CHIPS_X = 4


def along_x(step):
    pairs = []
    for i in range(NCTX):
        y, x, c = i // (2 * CHIPS_X), i // 2 % CHIPS_X, i % 2
        pairs.append((i, (y * CHIPS_X + (x + step) % CHIPS_X) * 2 + c))
    return pairs


def other_core(value):
    return lax.ppermute(value, "ctx", [(i, i ^ 1) for i in range(NCTX)])


def context_parts(x_in, b_in, c_in, decay_log, q_in, k_in, v_in, expert_out):
    me = lax.axis_index("ctx").astype(jnp.int32).reshape(1)
    chunks = chunks_to_send(x_in, b_in, decay_log, k_in, v_in)
    received = lax.all_to_all(chunks, "ctx", split_axis=0, concat_axis=0, tiled=True)
    blocks = expert_blocks(expert_out, chunks)
    own, entering = take_received(received, blocks[1:])
    half = NCTX // 2
    right = lax.ppermute(own, "ctx", along_x(1))
    left = lax.ppermute(own, "ctx", along_x(-1))
    far = jnp.concatenate(
        [
            lax.ppermute(right[:half], "ctx", along_x(1)),
            lax.ppermute(left[half:], "ctx", along_x(-1)),
        ]
    )
    near = jnp.concatenate([own, right, left])
    near_other = other_core(near)
    far_other = other_core(far)

    entering = lax.all_to_all(entering, "ctx", split_axis=0, concat_axis=0, tiled=True)
    local = local_part(x_in, b_in, c_in, decay_log)
    mamba_out = join_mamba(local, entering.reshape(MH * L, HD), c_in, decay_log)

    carry = attend(me, q_in, [k_in, v_in], [own, right, left])
    carry = attend(me, q_in, carry, [far, near_other])
    attn_out = attend(me, q_in, carry, [far_other], last=True)
    return mamba_out, attn_out, blocks


def blocks_kernel(me_ref, e_ref, after_ref, *outs):
    for d, o_ref in enumerate(outs):
        to = lax.rem(me_ref[0] + d, len(outs))
        o_ref[...] = jnp.concatenate(
            [e_ref[0, i, to].astype(F32) for i in range(e_ref.shape[1])], axis=0
        ).astype(BF16)


def combine_kernel(me_ref, ids_ref, idst_ref, gates_ref, *refs):
    rows_refs, o_ref = refs[:-1], refs[-1]
    peers = len(rows_refs)
    rows = jnp.concatenate([r[...].astype(F32) for r in rows_refs], axis=0).astype(BF16)
    owned = rows.shape[0] // (peers * CAP)
    count = ids_ref.shape[0]
    ids, idst, gates = ids_ref[...], idst_ref[...], gates_ref[...]
    t = lax.broadcasted_iota(jnp.int32, (count, count), 0)
    u = lax.broadcasted_iota(jnp.int32, (count, count), 1)
    place = lax.broadcasted_iota(jnp.int32, (count, rows.shape[0]), 1)
    out = None
    for k in range(2):
        mine = ids[:, k : k + 1]
        slot = jnp.zeros((count, 1), jnp.int32)
        for j in range(2):
            before = (u < t) if j >= k else (u <= t)
            same = jnp.logical_and(before, idst[j : j + 1, :] == mine)
            slot = slot + jnp.sum(same.astype(jnp.int32), axis=1, keepdims=True)
        distance = (me_ref[0] - mine // owned + peers) % peers
        number = (distance * owned + mine % owned) * CAP + slot
        pick = (place == number).astype(F32).astype(BF16)
        row = jnp.dot(pick, rows, preferred_element_type=F32)
        term = gates[:, k : k + 1] * row
        out = term if out is None else out + term
    o_ref[...] = out.astype(BF16)


def expert_blocks(expert_out, after):
    owned, peers, cap, width = expert_out.shape[1:]
    me = lax.axis_index("grp").astype(jnp.int32).reshape(1)
    held = pl.pallas_call(
        blocks_kernel,
        out_shape=[jax.ShapeDtypeStruct((owned * cap, width), BF16)] * peers,
        in_specs=[SM, VM, ANY],
        out_specs=[VM] * peers,
        compiler_params=params(),
        cost_estimate=cost(1 << 20, 1 << 21),
    )(me, expert_out, after)
    blocks = [held[0]]
    for d in range(1, peers):
        pairs = [(i, (i + d) % peers) for i in range(peers)]
        blocks.append(lax.ppermute(held[d], "grp", pairs))
    return blocks


def expert_part(expert_ids, gates, blocks):
    me = lax.axis_index("grp").astype(jnp.int32).reshape(1)
    peers = len(blocks)
    rows, width = blocks[0].shape
    count = expert_ids.shape[0]
    block = 2048
    return pl.pallas_call(
        combine_kernel,
        grid=(width // block,),
        out_shape=jax.ShapeDtypeStruct((count, width), BF16),
        in_specs=[
            SM,
            pl.BlockSpec((count, 2), lambda i: (0, 0)),
            pl.BlockSpec((2, count), lambda i: (0, 0)),
            pl.BlockSpec((count, 2), lambda i: (0, 0)),
        ]
        + [pl.BlockSpec((rows, block), lambda i: (0, i))] * peers,
        out_specs=pl.BlockSpec((count, block), lambda i: (0, i)),
        compiler_params=params(),
        cost_estimate=cost(1 << 24, 1 << 20),
    )(me, expert_ids, expert_ids.T, gates, *blocks)


def shards(x_in, b_in, c_in, decay_log, q_in, k_in, v_in, expert_ids, gates, expert_out):
    mamba_out, attn_out, blocks = context_parts(
        x_in, b_in, c_in, decay_log, q_in, k_in, v_in, expert_out
    )
    moe_out = expert_part(expert_ids, gates, blocks)
    return (mamba_out, attn_out, moe_out)


def solution(mesh):
    return jax.shard_map(
        shards,
        mesh=mesh,
        in_specs=(
            P("ctx", "grp"),
            P("ctx", None),
            P("ctx", None),
            P("grp", "ctx"),
            P("ctx", "grp"),
            P("ctx", "grp"),
            P("ctx", "grp"),
            P(("ctx", "grp"), None),
            P(("ctx", "grp"), None),
            P("ctx", "grp", None, None, None),
        ),
        out_specs=(P("ctx", "grp"), P("ctx", "grp"), P(("ctx", "grp"), None)),
        check_vma=False,
    )
```

```python
import math

import jax
import jax.numpy as jnp
from jax import lax
from jax.experimental import pallas as pl
from jax.experimental.pallas import tpu as pltpu
from jax.sharding import PartitionSpec as P

HD = 128
L = 128
MH = 16
NCTX = 64
QH = 4
CAP = 4
LOG2E = 1.4426950408889634
F32 = jnp.float32
BF16 = jnp.bfloat16
VM = pl.BlockSpec(memory_space=pltpu.VMEM)
SM = pl.BlockSpec(memory_space=pltpu.SMEM)
ANY = pl.BlockSpec(memory_space=pl.ANY)


LARGE, SMALL = 60, 16


def params(mib=SMALL):
    return pltpu.CompilerParams(vmem_limit_bytes=mib * 2**20)


def cost(flops, nbytes):
    return pl.CostEstimate(flops=flops, bytes_accessed=nbytes, transcendentals=0)


def tri(lower):
    r = lax.broadcasted_iota(jnp.int32, (L, L), 0)
    c = lax.broadcasted_iota(jnp.int32, (L, L), 1)
    return (c <= r) if lower else (r <= c)


def row_cumulative(decay):
    return jnp.dot(
        decay, tri(False).astype(F32), precision=lax.Precision.HIGHEST, preferred_element_type=F32
    )


def col_cumulative(decay):
    return lax.dot_general(
        tri(True).astype(F32),
        decay,
        (((1,), (1,)), ((), ())),
        precision=lax.Precision.HIGHEST,
        preferred_element_type=F32,
    )


PIECE = 16
KV = 2 * PIECE
SL = 32
CHUNK = KV + SL + 8


def send_kernel(x_ref, b_ref, d_ref, k_ref, v_ref, o_ref):
    cum = row_cumulative(d_ref[...])
    tail = jnp.exp(cum[:, L - 1 :] - cum)
    block_decay = jnp.exp(cum[:, L - 1 :])
    bt = b_ref[...].astype(F32).T
    row = lax.broadcasted_iota(jnp.int32, (8, L), 0)
    pieces = L // PIECE
    for h in range(MH):
        wb = (tail[h : h + 1, :] * bt).astype(BF16)
        s = jnp.dot(wb, x_ref[:, h * HD : (h + 1) * HD], preferred_element_type=F32)
        d = jnp.broadcast_to(block_decay[h : h + 1, :], (8, L))
        hi = d.astype(BF16).astype(F32)
        mid = (d - hi).astype(BF16).astype(F32)
        lo = d - hi - mid
        terms = jnp.where(row == 0, hi, jnp.where(row == 1, mid, jnp.where(row == 2, lo, 0.0)))
        for q in range(4):
            j = h * 4 + q
            rows = slice((j % pieces) * PIECE, (j % pieces + 1) * PIECE)
            o_ref[j, 0:PIECE, :] = k_ref[rows, :]
            o_ref[j, PIECE:KV, :] = v_ref[rows, :]
            o_ref[j, KV:CHUNK, :] = jnp.concatenate(
                [s[q * SL : (q + 1) * SL], terms], axis=0
            ).astype(BF16)


def chunks_to_send(x_in, b_in, decay_log, k_in, v_in):
    return pl.pallas_call(
        send_kernel,
        out_shape=jax.ShapeDtypeStruct((NCTX, CHUNK, HD), BF16),
        in_specs=[VM] * 5,
        out_specs=VM,
        compiler_params=params(LARGE),
        cost_estimate=cost(1 << 26, 1 << 21),
    )(x_in, b_in, decay_log, k_in, v_in)


def take_kernel(s_ref, *refs):
    own_ref, o_ref = refs[-2:]
    own_ref[...] = s_ref[:, :KV, :]

    def step(k, e):
        o_ref[k] = e.astype(BF16)
        block = s_ref[k, KV:CHUNK, :].astype(F32)
        d = block[SL : SL + 1] + block[SL + 1 : SL + 2] + block[SL + 2 : SL + 3]
        return d * e + block[:SL]

    lax.fori_loop(0, NCTX, step, jnp.zeros((SL, HD), F32), unroll=8)


def take_received(received, after):
    return pl.pallas_call(
        take_kernel,
        out_shape=[
            jax.ShapeDtypeStruct((NCTX, KV, HD), BF16),
            jax.ShapeDtypeStruct((NCTX, SL, HD), BF16),
        ],
        in_specs=[VM] + [ANY] * len(after),
        out_specs=[VM, VM],
        compiler_params=params(),
        cost_estimate=cost(1 << 20, 1 << 21),
    )(received, *after)


def local_kernel(x_ref, b_ref, c_ref, d_ref, o_ref):
    cum = row_cumulative(d_ref[...])
    cum_col = col_cumulative(d_ref[...])
    cross = lax.dot_general(
        c_ref[...], b_ref[...], (((1,), (1,)), ((), ())), preferred_element_type=F32
    )
    mask = tri(True)
    for h in range(MH):
        gap = jnp.where(mask, cum_col[:, h : h + 1] - cum[h : h + 1, :], -1e30)
        w = (jnp.exp(gap) * cross).astype(BF16)
        o_ref[:, h * HD : (h + 1) * HD] = jnp.dot(
            w, x_ref[:, h * HD : (h + 1) * HD], preferred_element_type=F32
        )


def local_part(x_in, b_in, c_in, decay_log):
    return pl.pallas_call(
        local_kernel,
        out_shape=jax.ShapeDtypeStruct((L, MH * HD), F32),
        in_specs=[VM] * 4,
        out_specs=VM,
        compiler_params=params(LARGE),
        cost_estimate=cost(1 << 28, 1 << 21),
    )(x_in, b_in, c_in, decay_log)


JOIN_COST = 1 << 35


def join_kernel(l_ref, e_ref, c_ref, d_ref, *refs):
    o_ref = refs[-1]
    grow = jnp.exp(col_cumulative(d_ref[...]))
    c = c_ref[...]
    for h in range(MH):
        cols = slice(h * HD, (h + 1) * HD)
        readout = jnp.dot(c, e_ref[cols, :], preferred_element_type=F32)
        o_ref[:, cols] = (l_ref[:, cols] + grow[:, h : h + 1] * readout).astype(BF16)


def join_mamba(local, entering, c_in, decay_log, after):
    return pl.pallas_call(
        join_kernel,
        out_shape=jax.ShapeDtypeStruct((L, MH * HD), BF16),
        in_specs=[VM] * 4 + [ANY] * len(after),
        out_specs=VM,
        compiler_params=params(),
        cost_estimate=cost(JOIN_COST, 1 << 21),
    )(local, entering, c_in, decay_log, *after)


ROWS = QH * L
SCALE2 = LOG2E / math.sqrt(HD)


def stacked_queries(q_ref):
    return jnp.concatenate([q_ref[:, g * HD : (g + 1) * HD] for g in range(QH)], axis=0)


def accumulate(state, s, v):
    m_old, total, acc = state
    m = jnp.maximum(m_old, jnp.max(s, axis=1, keepdims=True))
    factor = jnp.exp2((m_old - m) * SCALE2)
    p = jnp.exp2((s - m) * SCALE2)
    part = p[:, :L]
    for j in range(1, p.shape[1] // L):
        part = part + p[:, j * L : (j + 1) * L]
    added = jnp.dot(p.astype(BF16), v, preferred_element_type=F32)
    return m, total * factor + part, acc * factor + added


def scores(q, k):
    return lax.dot_general(q, k, (((1,), (1,)), ((), ())), preferred_element_type=F32)


def open_kernel(q_ref, k_ref, v_ref, s_ref, m_ref, l_ref, a_ref):
    q = stacked_queries(q_ref)
    s_ref[...] = q
    s = scores(q, k_ref[...])
    t = lax.broadcasted_iota(jnp.int32, s.shape, 0) % L
    u = lax.broadcasted_iota(jnp.int32, s.shape, 1)
    s = jnp.where(u <= t, s, -1e30)
    m = jnp.max(s, axis=1, keepdims=True)
    p = jnp.exp2((s - m) * SCALE2)
    m_ref[...] = jnp.broadcast_to(m, (ROWS, L))
    l_ref[...] = p
    a_ref[...] = jnp.dot(p.astype(BF16), v_ref[...], preferred_element_type=F32)


def open_attention(q_in, k_in, v_in):
    return pl.pallas_call(
        open_kernel,
        out_shape=[jax.ShapeDtypeStruct((ROWS, HD), BF16)]
        + [jax.ShapeDtypeStruct((ROWS, L), F32)] * 3,
        in_specs=[VM] * 3,
        out_specs=[VM] * 4,
        compiler_params=params(LARGE),
        cost_estimate=cost(1 << 27, 1 << 20),
    )(q_in, k_in, v_in)


def attend_kernel(n_sets, last, me_ref, q_ref, m_in, l_in, a_in, *refs):
    sets, refs = refs[:n_sets], refs[n_sets:]
    if last:
        o_ref, m_ref, l_ref, a_ref = refs
    else:
        m_ref, l_ref, a_ref = refs
    me = me_ref[0]
    q = q_ref[...]
    m_ref[...] = m_in[...]
    l_ref[...] = l_in[...]
    a_ref[...] = a_in[...]
    keys = NCTX * PIECE
    shard = lax.broadcasted_iota(jnp.int32, (1, keys), 1) // PIECE
    bias = jnp.where(shard < me, 0.0, -1e30)
    for ref in sets:
        for at in range(ref.shape[0] // NCTX):
            pick = slice(at * NCTX, (at + 1) * NCTX)
            k = ref[pick, 0:PIECE, :].reshape(keys, HD)
            v = ref[pick, PIECE:KV, :].reshape(keys, HD)
            s = scores(q, k) + bias
            m, total, acc = accumulate((m_ref[:, :1], l_ref[...], a_ref[...]), s, v)
            m_ref[...] = jnp.broadcast_to(m, (ROWS, L))
            l_ref[...] = total
            a_ref[...] = acc
    if last:
        out = a_ref[...] / jnp.sum(l_ref[...], axis=1, keepdims=True)
        for g in range(QH):
            o_ref[:, g * HD : (g + 1) * HD] = out[g * L : (g + 1) * L].astype(BF16)


def attend(me, queries, carry, sets, last=False):
    after = [jax.ShapeDtypeStruct((ROWS, L), F32)] * 3

    def kernel(*refs):
        attend_kernel(len(sets), last, *refs)

    return pl.pallas_call(
        kernel,
        out_shape=jax.ShapeDtypeStruct((L, QH * HD), BF16) if last else after,
        in_specs=[SM] + [VM] * (4 + len(sets)),
        out_specs=VM if last else [VM] * 3,
        scratch_shapes=[pltpu.VMEM((ROWS, L), F32)] * 3 if last else [],
        compiler_params=params(),
        cost_estimate=cost(1 << 28, len(sets) << 22),
    )(me, queries, *carry, *sets)


CHIPS_X = 4


def along_x(step):
    pairs = []
    for i in range(NCTX):
        y, x, c = i // (2 * CHIPS_X), i // 2 % CHIPS_X, i % 2
        pairs.append((i, (y * CHIPS_X + (x + step) % CHIPS_X) * 2 + c))
    return pairs


def other_core(value):
    return lax.ppermute(value, "ctx", [(i, i ^ 1) for i in range(NCTX)])


def context_parts(x_in, b_in, c_in, decay_log, q_in, k_in, v_in, expert_out):
    me = lax.axis_index("ctx").astype(jnp.int32).reshape(1)
    chunks = chunks_to_send(x_in, b_in, decay_log, k_in, v_in)
    queries, *carry = open_attention(q_in, k_in, v_in)
    received = lax.all_to_all(chunks, "ctx", split_axis=0, concat_axis=0, tiled=True)
    blocks = expert_blocks(expert_out, chunks)
    local = local_part(x_in, b_in, c_in, decay_log)
    sooner = [blocks[d] for d in (1, 7, 2, 6) if d < len(blocks)]
    own, entering = take_received(received, [local, queries, *sooner])
    half = NCTX // 2
    right = lax.ppermute(own, "ctx", along_x(1))
    left = lax.ppermute(own, "ctx", along_x(-1))
    far = jnp.concatenate(
        [
            lax.ppermute(right[:half], "ctx", along_x(1)),
            lax.ppermute(left[half:], "ctx", along_x(-1)),
        ]
    )
    near = jnp.concatenate([own, right, left])
    near_other = other_core(near)
    far_other = other_core(far)

    entering = lax.all_to_all(entering, "ctx", split_axis=0, concat_axis=0, tiled=True)
    later = [blocks[d] for d in (3, 5, 4) if d < len(blocks)]
    mamba_out = join_mamba(local, entering.reshape(MH * L, HD), c_in, decay_log, later)

    carry = attend(me, queries, carry, [own, right, left])
    carry = attend(me, queries, carry, [far, near_other])
    attn_out = attend(me, queries, carry, [far_other], last=True)
    return mamba_out, attn_out, blocks


def blocks_kernel(me_ref, e_ref, after_ref, *outs):
    for d, o_ref in enumerate(outs):
        to = lax.rem(me_ref[0] + d, len(outs))
        o_ref[...] = jnp.concatenate(
            [e_ref[0, i, to].astype(F32) for i in range(e_ref.shape[1])], axis=0
        ).astype(BF16)


def combine_kernel(me_ref, ids_ref, idst_ref, gates_ref, *refs):
    rows_refs, o_ref = refs[:-2], refs[-1]
    peers = len(rows_refs)
    rows = jnp.concatenate([r[...].astype(F32) for r in rows_refs], axis=0).astype(BF16)
    owned = rows.shape[0] // (peers * CAP)
    count = ids_ref.shape[0]
    ids, idst, gates = ids_ref[...], idst_ref[...], gates_ref[...]
    t = lax.broadcasted_iota(jnp.int32, (count, count), 0)
    u = lax.broadcasted_iota(jnp.int32, (count, count), 1)
    place = lax.broadcasted_iota(jnp.int32, (count, rows.shape[0]), 1)
    out = None
    for k in range(2):
        mine = ids[:, k : k + 1]
        slot = jnp.zeros((count, 1), jnp.int32)
        for j in range(2):
            before = (u < t) if j >= k else (u <= t)
            same = jnp.logical_and(before, idst[j : j + 1, :] == mine)
            slot = slot + jnp.sum(same.astype(jnp.int32), axis=1, keepdims=True)
        distance = (me_ref[0] - mine // owned + peers) % peers
        number = (distance * owned + mine % owned) * CAP + slot
        pick = (place == number).astype(F32).astype(BF16)
        row = jnp.dot(pick, rows, preferred_element_type=F32)
        term = gates[:, k : k + 1] * row
        out = term if out is None else out + term
    o_ref[...] = out.astype(BF16)


def expert_blocks(expert_out, after):
    owned, peers, cap, width = expert_out.shape[1:]
    me = lax.axis_index("grp").astype(jnp.int32).reshape(1)
    held = pl.pallas_call(
        blocks_kernel,
        out_shape=[jax.ShapeDtypeStruct((owned * cap, width), BF16)] * peers,
        in_specs=[SM, VM, ANY],
        out_specs=[VM] * peers,
        compiler_params=params(LARGE),
        cost_estimate=cost(1 << 20, 1 << 21),
    )(me, expert_out, after)
    blocks = [held[0]]
    for d in range(1, peers):
        pairs = [(i, (i + d) % peers) for i in range(peers)]
        blocks.append(lax.ppermute(held[d], "grp", pairs))
    return blocks


def expert_part(expert_ids, gates, blocks, after):
    me = lax.axis_index("grp").astype(jnp.int32).reshape(1)
    peers = len(blocks)
    rows, width = blocks[0].shape
    count = expert_ids.shape[0]
    block = 2048
    return pl.pallas_call(
        combine_kernel,
        grid=(width // block,),
        out_shape=jax.ShapeDtypeStruct((count, width), BF16),
        in_specs=[
            SM,
            pl.BlockSpec((count, 2), lambda i: (0, 0)),
            pl.BlockSpec((2, count), lambda i: (0, 0)),
            pl.BlockSpec((count, 2), lambda i: (0, 0)),
        ]
        + [pl.BlockSpec((rows, block), lambda i: (0, i))] * peers
        + [ANY],
        out_specs=pl.BlockSpec((count, block), lambda i: (0, i)),
        compiler_params=params(),
        cost_estimate=cost(1 << 24, 1 << 20),
    )(me, expert_ids, expert_ids.T, gates, *blocks, after)


def shards(x_in, b_in, c_in, decay_log, q_in, k_in, v_in, expert_ids, gates, expert_out):
    mamba_out, attn_out, blocks = context_parts(
        x_in, b_in, c_in, decay_log, q_in, k_in, v_in, expert_out
    )
    moe_out = expert_part(expert_ids, gates, blocks, mamba_out)
    return (mamba_out, attn_out, moe_out)


def solution(mesh):
    return jax.shard_map(
        shards,
        mesh=mesh,
        in_specs=(
            P("ctx", "grp"),
            P("ctx", None),
            P("ctx", None),
            P("grp", "ctx"),
            P("ctx", "grp"),
            P("ctx", "grp"),
            P("ctx", "grp"),
            P(("ctx", "grp"), None),
            P(("ctx", "grp"), None),
            P("ctx", "grp", None, None, None),
        ),
        out_specs=(P("ctx", "grp"), P("ctx", "grp"), P(("ctx", "grp"), None)),
        check_vma=False,
    )
```

```python
import math

import jax
import jax.numpy as jnp
from jax import lax
from jax.experimental import pallas as pl
from jax.experimental.pallas import tpu as pltpu
from jax.sharding import PartitionSpec as P

HD = 128
L = 128
MH = 16
NCTX = 64
QH = 4
CAP = 4
LOG2E = 1.4426950408889634
F32 = jnp.float32
BF16 = jnp.bfloat16
VM = pl.BlockSpec(memory_space=pltpu.VMEM)
SM = pl.BlockSpec(memory_space=pltpu.SMEM)
ANY = pl.BlockSpec(memory_space=pl.ANY)


LARGE, SMALL = 60, 24


def params(mib=SMALL):
    return pltpu.CompilerParams(vmem_limit_bytes=mib * 2**20)


def cost(flops, nbytes):
    return pl.CostEstimate(flops=flops, bytes_accessed=nbytes, transcendentals=0)


def tri(lower):
    r = lax.broadcasted_iota(jnp.int32, (L, L), 0)
    c = lax.broadcasted_iota(jnp.int32, (L, L), 1)
    return (c <= r) if lower else (r <= c)


def row_cumulative(decay):
    return jnp.dot(
        decay, tri(False).astype(F32), precision=lax.Precision.HIGHEST, preferred_element_type=F32
    )


def col_cumulative(decay):
    return lax.dot_general(
        tri(True).astype(F32),
        decay,
        (((1,), (1,)), ((), ())),
        precision=lax.Precision.HIGHEST,
        preferred_element_type=F32,
    )


PIECE = 16
KV = 2 * PIECE
SL = 32
CHUNK = 2 * KV + SL + 8


def send_kernel(x_ref, b_ref, d_ref, k_ref, v_ref, o_ref):
    cum = row_cumulative(d_ref[...])
    tail = jnp.exp(cum[:, L - 1 :] - cum)
    block_decay = jnp.exp(cum[:, L - 1 :])
    bt = b_ref[...].astype(F32).T
    row = lax.broadcasted_iota(jnp.int32, (8, L), 0)
    pieces = L // PIECE
    for h in range(MH):
        wb = (tail[h : h + 1, :] * bt).astype(BF16)
        s = jnp.dot(wb, x_ref[:, h * HD : (h + 1) * HD], preferred_element_type=F32)
        d = jnp.broadcast_to(block_decay[h : h + 1, :], (8, L))
        hi = d.astype(BF16).astype(F32)
        mid = (d - hi).astype(BF16).astype(F32)
        lo = d - hi - mid
        terms = jnp.where(row == 0, hi, jnp.where(row == 1, mid, jnp.where(row == 2, lo, 0.0)))
        for q in range(4):
            j = h * 4 + q
            for turn in range(2):
                at = (j + turn * pieces // 2) % pieces * PIECE
                o_ref[j, turn * KV : turn * KV + PIECE, :] = k_ref[at : at + PIECE, :]
                o_ref[j, turn * KV + PIECE : (turn + 1) * KV, :] = v_ref[at : at + PIECE, :]
            o_ref[j, 2 * KV : CHUNK, :] = jnp.concatenate(
                [s[q * SL : (q + 1) * SL], terms], axis=0
            ).astype(BF16)


def chunks_to_send(x_in, b_in, decay_log, k_in, v_in):
    return pl.pallas_call(
        send_kernel,
        out_shape=jax.ShapeDtypeStruct((NCTX, CHUNK, HD), BF16),
        in_specs=[VM] * 5,
        out_specs=VM,
        compiler_params=params(LARGE),
        cost_estimate=cost(1 << 26, 1 << 21),
    )(x_in, b_in, decay_log, k_in, v_in)


def take_kernel(s_ref, *refs):
    own_ref, opposite_ref, o_ref = refs[-3:]
    own_ref[...] = s_ref[:, :KV, :]
    opposite_ref[...] = s_ref[:, KV : 2 * KV, :]

    def step(k, e):
        o_ref[k] = e.astype(BF16)
        block = s_ref[k, 2 * KV : CHUNK, :].astype(F32)
        d = block[SL : SL + 1] + block[SL + 1 : SL + 2] + block[SL + 2 : SL + 3]
        return d * e + block[:SL]

    lax.fori_loop(0, NCTX, step, jnp.zeros((SL, HD), F32), unroll=8)


def take_received(received, after):
    return pl.pallas_call(
        take_kernel,
        out_shape=[
            jax.ShapeDtypeStruct((NCTX, KV, HD), BF16),
            jax.ShapeDtypeStruct((NCTX, KV, HD), BF16),
            jax.ShapeDtypeStruct((NCTX, SL, HD), BF16),
        ],
        in_specs=[VM] + [ANY] * len(after),
        out_specs=[VM] * 3,
        compiler_params=params(),
        cost_estimate=cost(1 << 20, 1 << 21),
    )(received, *after)


def local_kernel(x_ref, b_ref, c_ref, d_ref, o_ref):
    cum = row_cumulative(d_ref[...])
    cum_col = col_cumulative(d_ref[...])
    cross = lax.dot_general(
        c_ref[...], b_ref[...], (((1,), (1,)), ((), ())), preferred_element_type=F32
    )
    mask = tri(True)
    for h in range(MH):
        gap = jnp.where(mask, cum_col[:, h : h + 1] - cum[h : h + 1, :], -1e30)
        w = (jnp.exp(gap) * cross).astype(BF16)
        o_ref[:, h * HD : (h + 1) * HD] = jnp.dot(
            w, x_ref[:, h * HD : (h + 1) * HD], preferred_element_type=F32
        )


def local_part(x_in, b_in, c_in, decay_log):
    return pl.pallas_call(
        local_kernel,
        out_shape=jax.ShapeDtypeStruct((L, MH * HD), F32),
        in_specs=[VM] * 4,
        out_specs=VM,
        compiler_params=params(LARGE),
        cost_estimate=cost(1 << 28, 1 << 21),
    )(x_in, b_in, c_in, decay_log)


JOIN_COST = 1 << 35


def join_kernel(l_ref, e_ref, c_ref, d_ref, o_ref):
    grow = jnp.exp(col_cumulative(d_ref[...]))
    c = c_ref[...]
    for h in range(MH):
        cols = slice(h * HD, (h + 1) * HD)
        readout = jnp.dot(c, e_ref[cols, :], preferred_element_type=F32)
        o_ref[:, cols] = (l_ref[:, cols] + grow[:, h : h + 1] * readout).astype(BF16)


def join_mamba(local, entering, c_in, decay_log):
    return pl.pallas_call(
        join_kernel,
        out_shape=jax.ShapeDtypeStruct((L, MH * HD), BF16),
        in_specs=[VM] * 4,
        out_specs=VM,
        compiler_params=params(),
        cost_estimate=cost(JOIN_COST, 1 << 21),
    )(local, entering, c_in, decay_log)


ROWS = QH * L
SCALE2 = LOG2E / math.sqrt(HD)


def stacked_queries(q_ref):
    return jnp.concatenate([q_ref[:, g * HD : (g + 1) * HD] for g in range(QH)], axis=0)


def accumulate(state, s, v):
    m_old, total, acc = state
    m = jnp.maximum(m_old, jnp.max(s, axis=1, keepdims=True))
    factor = jnp.exp2((m_old - m) * SCALE2)
    p = jnp.exp2((s - m) * SCALE2)
    part = p[:, :L]
    for j in range(1, p.shape[1] // L):
        part = part + p[:, j * L : (j + 1) * L]
    added = jnp.dot(p.astype(BF16), v, preferred_element_type=F32)
    return m, total * factor + part, acc * factor + added


def scores(q, k):
    return lax.dot_general(q, k, (((1,), (1,)), ((), ())), preferred_element_type=F32)


def open_kernel(q_ref, q2_ref, k_ref, v_ref, s_ref, s2_ref, m_ref, l_ref, a_ref):
    q = stacked_queries(q_ref)
    s_ref[...] = q
    s2_ref[...] = stacked_queries(q2_ref)
    s = scores(q, k_ref[...])
    t = lax.broadcasted_iota(jnp.int32, s.shape, 0) % L
    u = lax.broadcasted_iota(jnp.int32, s.shape, 1)
    s = jnp.where(u <= t, s, -1e30)
    m = jnp.max(s, axis=1, keepdims=True)
    p = jnp.exp2((s - m) * SCALE2)
    m_ref[...] = jnp.broadcast_to(m, (ROWS, L))
    l_ref[...] = p
    a_ref[...] = jnp.dot(p.astype(BF16), v_ref[...], preferred_element_type=F32)


PART = jax.ShapeDtypeStruct((ROWS, L), F32)


def open_attention(q_in, q_other, k_in, v_in):
    return pl.pallas_call(
        open_kernel,
        out_shape=[jax.ShapeDtypeStruct((ROWS, HD), BF16)] * 2 + [PART] * 3,
        in_specs=[VM] * 4,
        out_specs=[VM] * 5,
        compiler_params=params(LARGE),
        cost_estimate=cost(1 << 27, 1 << 20),
    )(q_in, q_other, k_in, v_in)


def attend_kernel(n_sets, fresh, pack, other, me_ref, q_ref, *refs):
    if not fresh:
        m_in, l_in, a_in = refs[:3]
        refs = refs[3:]
    sets, refs = refs[:n_sets], refs[n_sets:]
    if pack:
        o_ref, m_ref, l_ref, a_ref = refs
    else:
        m_ref, l_ref, a_ref = refs
    me = (me_ref[0] ^ 1) if other else me_ref[0]
    q = q_ref[...]
    if fresh:
        m_ref[...] = jnp.full((ROWS, L), -1e30, F32)
        l_ref[...] = jnp.zeros((ROWS, L), F32)
        a_ref[...] = jnp.zeros((ROWS, HD), F32)
    else:
        m_ref[...] = m_in[...]
        l_ref[...] = l_in[...]
        a_ref[...] = a_in[...]
    keys = NCTX * PIECE
    shard = lax.broadcasted_iota(jnp.int32, (1, keys), 1) // PIECE
    bias = jnp.where(shard < me, 0.0, -1e30)

    @pl.when(me > 0)
    def _():
        for ref in sets:
            k = ref[:, 0:PIECE, :].reshape(keys, HD)
            v = ref[:, PIECE:KV, :].reshape(keys, HD)
            s = scores(q, k) + bias
            m, total, acc = accumulate((m_ref[:, :1], l_ref[...], a_ref[...]), s, v)
            m_ref[...] = jnp.broadcast_to(m, (ROWS, L))
            l_ref[...] = total
            a_ref[...] = acc

    if pack:
        lane = lax.broadcasted_iota(jnp.int32, (ROWS, L), 1)
        total = jnp.sum(l_ref[...], axis=1, keepdims=True)
        o_ref[:, :HD] = a_ref[...]
        o_ref[:, HD:] = jnp.where(lane < L // 2, m_ref[...], total)


def attend(me, queries, carry, sets, other=False, pack=False):
    def kernel(*refs):
        attend_kernel(len(sets), not carry, pack, other, *refs)

    return pl.pallas_call(
        kernel,
        out_shape=jax.ShapeDtypeStruct((ROWS, HD + L), F32) if pack else [PART] * 3,
        in_specs=[SM] + [VM] * (1 + len(carry) + len(sets)),
        out_specs=VM if pack else [VM] * 3,
        scratch_shapes=[pltpu.VMEM((ROWS, L), F32)] * 3 if pack else [],
        compiler_params=params(),
        cost_estimate=cost(1 << 28, len(sets) << 20),
    )(me, queries, *carry, *sets)


def merge_kernel(m_ref, l_ref, a_ref, p_ref, o_ref):
    m1, m2 = m_ref[:, :1], p_ref[:, HD : HD + 1]
    m = jnp.maximum(m1, m2)
    f1, f2 = jnp.exp2((m1 - m) * SCALE2), jnp.exp2((m2 - m) * SCALE2)
    total = jnp.sum(l_ref[...], axis=1, keepdims=True) * f1 + p_ref[:, HD + L - 1 :] * f2
    out = (a_ref[...] * f1 + p_ref[:, :HD] * f2) / total
    for g in range(QH):
        o_ref[:, g * HD : (g + 1) * HD] = out[g * L : (g + 1) * L].astype(BF16)


def merge_attention(carry, part):
    return pl.pallas_call(
        merge_kernel,
        out_shape=jax.ShapeDtypeStruct((L, QH * HD), BF16),
        in_specs=[VM] * 4,
        out_specs=VM,
        compiler_params=params(),
        cost_estimate=cost(1 << 20, 1 << 20),
    )(*carry, part)


CHIPS_X = 4


def along_x(step):
    pairs = []
    for i in range(NCTX):
        y, x, c = i // (2 * CHIPS_X), i // 2 % CHIPS_X, i % 2
        pairs.append((i, (y * CHIPS_X + (x + step) % CHIPS_X) * 2 + c))
    return pairs


def other_core(value):
    return lax.ppermute(value, "ctx", [(i, i ^ 1) for i in range(NCTX)])


def context_parts(x_in, b_in, c_in, decay_log, q_in, k_in, v_in, expert_out):
    me = lax.axis_index("ctx").astype(jnp.int32).reshape(1)
    chunks = chunks_to_send(x_in, b_in, decay_log, k_in, v_in)
    received = lax.all_to_all(chunks, "ctx", split_axis=0, concat_axis=0, tiled=True)
    blocks = expert_blocks(expert_out, chunks)
    q_other = other_core(q_in)
    q_own, q_other, *carry = open_attention(q_in, q_other, k_in, v_in)
    local = local_part(x_in, b_in, c_in, decay_log)
    own, opposite, entering = take_received(received, [local, q_own, *blocks[1:]])
    right = lax.ppermute(own, "ctx", along_x(1))
    left = lax.ppermute(own, "ctx", along_x(-1))

    entering = lax.all_to_all(entering, "ctx", split_axis=0, concat_axis=0, tiled=True)
    mamba_out = join_mamba(local, entering.reshape(MH * L, HD), c_in, decay_log)

    carry = attend(me, q_own, carry, [own, opposite])
    carry_other = attend(me, q_other, [], [own, opposite], other=True)
    part = attend(me, q_other, carry_other, [right, left], other=True, pack=True)
    part = other_core(part)
    carry = attend(me, q_own, carry, [right, left])
    return mamba_out, merge_attention(carry, part), blocks


def blocks_kernel(me_ref, e_ref, after_ref, *outs):
    for d, o_ref in enumerate(outs):
        to = lax.rem(me_ref[0] + d, len(outs))
        o_ref[...] = jnp.concatenate(
            [e_ref[0, i, to].astype(F32) for i in range(e_ref.shape[1])], axis=0
        ).astype(BF16)


def combine_kernel(me_ref, ids_ref, idst_ref, gates_ref, *refs):
    rows_refs, o_ref = refs[:-1], refs[-1]
    peers = len(rows_refs)
    rows = jnp.concatenate([r[...].astype(F32) for r in rows_refs], axis=0).astype(BF16)
    owned = rows.shape[0] // (peers * CAP)
    count = ids_ref.shape[0]
    ids, idst, gates = ids_ref[...], idst_ref[...], gates_ref[...]
    t = lax.broadcasted_iota(jnp.int32, (count, count), 0)
    u = lax.broadcasted_iota(jnp.int32, (count, count), 1)
    place = lax.broadcasted_iota(jnp.int32, (count, rows.shape[0]), 1)
    out = None
    for k in range(2):
        mine = ids[:, k : k + 1]
        slot = jnp.zeros((count, 1), jnp.int32)
        for j in range(2):
            before = (u < t) if j >= k else (u <= t)
            same = jnp.logical_and(before, idst[j : j + 1, :] == mine)
            slot = slot + jnp.sum(same.astype(jnp.int32), axis=1, keepdims=True)
        distance = (me_ref[0] - mine // owned + peers) % peers
        number = (distance * owned + mine % owned) * CAP + slot
        pick = (place == number).astype(F32).astype(BF16)
        row = jnp.dot(pick, rows, preferred_element_type=F32)
        term = gates[:, k : k + 1] * row
        out = term if out is None else out + term
    o_ref[...] = out.astype(BF16)


def expert_blocks(expert_out, after):
    owned, peers, cap, width = expert_out.shape[1:]
    me = lax.axis_index("grp").astype(jnp.int32).reshape(1)
    held = pl.pallas_call(
        blocks_kernel,
        out_shape=[jax.ShapeDtypeStruct((owned * cap, width), BF16)] * peers,
        in_specs=[SM, VM, ANY],
        out_specs=[VM] * peers,
        compiler_params=params(LARGE),
        cost_estimate=cost(1 << 20, 1 << 21),
    )(me, expert_out, after)
    blocks = list(held)
    for d in sorted(range(1, peers), key=lambda d: -min(d, peers - d)):
        pairs = [(i, (i + d) % peers) for i in range(peers)]
        blocks[d] = lax.ppermute(held[d], "grp", pairs)
    return blocks


def expert_part(expert_ids, gates, blocks):
    me = lax.axis_index("grp").astype(jnp.int32).reshape(1)
    peers = len(blocks)
    rows, width = blocks[0].shape
    count = expert_ids.shape[0]
    block = 2048
    return pl.pallas_call(
        combine_kernel,
        grid=(width // block,),
        out_shape=jax.ShapeDtypeStruct((count, width), BF16),
        in_specs=[
            SM,
            pl.BlockSpec((count, 2), lambda i: (0, 0)),
            pl.BlockSpec((2, count), lambda i: (0, 0)),
            pl.BlockSpec((count, 2), lambda i: (0, 0)),
        ]
        + [pl.BlockSpec((rows, block), lambda i: (0, i))] * peers,
        out_specs=pl.BlockSpec((count, block), lambda i: (0, i)),
        compiler_params=params(),
        cost_estimate=cost(1 << 24, 1 << 20),
    )(me, expert_ids, expert_ids.T, gates, *blocks)


def shards(x_in, b_in, c_in, decay_log, q_in, k_in, v_in, expert_ids, gates, expert_out):
    mamba_out, attn_out, blocks = context_parts(
        x_in, b_in, c_in, decay_log, q_in, k_in, v_in, expert_out
    )
    moe_out = expert_part(expert_ids, gates, blocks)
    return (mamba_out, attn_out, moe_out)


def solution(mesh):
    return jax.shard_map(
        shards,
        mesh=mesh,
        in_specs=(
            P("ctx", "grp"),
            P("ctx", None),
            P("ctx", None),
            P("grp", "ctx"),
            P("ctx", "grp"),
            P("ctx", "grp"),
            P("ctx", "grp"),
            P(("ctx", "grp"), None),
            P(("ctx", "grp"), None),
            P("ctx", "grp", None, None, None),
        ),
        out_specs=(P("ctx", "grp"), P("ctx", "grp"), P(("ctx", "grp"), None)),
        check_vma=False,
    )
```

```python
import math

import jax
import jax.numpy as jnp
from jax import lax
from jax.experimental import pallas as pl
from jax.experimental.pallas import tpu as pltpu
from jax.sharding import PartitionSpec as P

HD = 128
L = 128
MH = 16
NCTX = 64
QH = 4
CAP = 4
LOG2E = 1.4426950408889634
F32 = jnp.float32
BF16 = jnp.bfloat16
VM = pl.BlockSpec(memory_space=pltpu.VMEM)
SM = pl.BlockSpec(memory_space=pltpu.SMEM)
TILE = pl.BlockSpec((8, 128), lambda i: (0, 0))


LARGE, SMALL = 60, 24


def params(mib=SMALL):
    return pltpu.CompilerParams(vmem_limit_bytes=mib * 2**20)


def full(shape):
    return pl.BlockSpec(shape, lambda i: (0,) * len(shape))


def cost(flops, nbytes):
    return pl.CostEstimate(flops=flops, bytes_accessed=nbytes, transcendentals=0)


def tri(lower):
    r = lax.broadcasted_iota(jnp.int32, (L, L), 0)
    c = lax.broadcasted_iota(jnp.int32, (L, L), 1)
    return (c <= r) if lower else (r <= c)


def row_cumulative(decay):
    return jnp.dot(
        decay, tri(False).astype(F32), precision=lax.Precision.HIGHEST, preferred_element_type=F32
    )


def col_cumulative(decay):
    return lax.dot_general(
        tri(True).astype(F32),
        decay,
        (((1,), (1,)), ((), ())),
        precision=lax.Precision.HIGHEST,
        preferred_element_type=F32,
    )


PIECE = 16
KV = 2 * PIECE
SL = 32
CHUNK = 2 * KV + SL + 8


def send_kernel(x_ref, b_ref, d_ref, k_ref, v_ref, o_ref):
    cum = row_cumulative(d_ref[...])
    tail = jnp.exp(cum[:, L - 1 :] - cum)
    block_decay = jnp.exp(cum[:, L - 1 :])
    bt = b_ref[...].astype(F32).T
    row = lax.broadcasted_iota(jnp.int32, (8, L), 0)
    pieces = L // PIECE
    for h in range(MH):
        wb = (tail[h : h + 1, :] * bt).astype(BF16)
        s = jnp.dot(wb, x_ref[:, h * HD : (h + 1) * HD], preferred_element_type=F32)
        d = jnp.broadcast_to(block_decay[h : h + 1, :], (8, L))
        hi = d.astype(BF16).astype(F32)
        mid = (d - hi).astype(BF16).astype(F32)
        lo = d - hi - mid
        terms = jnp.where(row == 0, hi, jnp.where(row == 1, mid, jnp.where(row == 2, lo, 0.0)))
        for q in range(4):
            j = h * 4 + q
            for turn in range(2):
                at = (j + turn * pieces // 2) % pieces * PIECE
                o_ref[j, turn * KV : turn * KV + PIECE, :] = k_ref[at : at + PIECE, :]
                o_ref[j, turn * KV + PIECE : (turn + 1) * KV, :] = v_ref[at : at + PIECE, :]
            o_ref[j, 2 * KV : CHUNK, :] = jnp.concatenate(
                [s[q * SL : (q + 1) * SL], terms], axis=0
            ).astype(BF16)


def chunks_to_send(x_in, b_in, decay_log, k_in, v_in):
    return pl.pallas_call(
        send_kernel,
        out_shape=jax.ShapeDtypeStruct((NCTX, CHUNK, HD), BF16),
        in_specs=[VM] * 5,
        out_specs=VM,
        compiler_params=params(LARGE),
        cost_estimate=cost(1 << 26, 1 << 21),
    )(x_in, b_in, decay_log, k_in, v_in)


def take_kernel(s_ref, *refs):
    own_ref, opposite_ref, o_ref = refs[-3:]
    own_ref[...] = s_ref[:, :KV, :]
    opposite_ref[...] = s_ref[:, KV : 2 * KV, :]

    def step(k, e):
        o_ref[k] = e.astype(BF16)
        block = s_ref[k, 2 * KV : CHUNK, :].astype(F32)
        d = block[SL : SL + 1] + block[SL + 1 : SL + 2] + block[SL + 2 : SL + 3]
        return d * e + block[:SL]

    lax.fori_loop(0, NCTX, step, jnp.zeros((SL, HD), F32), unroll=8)


def take_received(received, after):
    return pl.pallas_call(
        take_kernel,
        out_shape=[
            jax.ShapeDtypeStruct((NCTX, KV, HD), BF16),
            jax.ShapeDtypeStruct((NCTX, KV, HD), BF16),
            jax.ShapeDtypeStruct((NCTX, SL, HD), BF16),
        ],
        grid=(1,),
        in_specs=[full(received.shape)] + [TILE] * len(after),
        out_specs=[full((NCTX, KV, HD)), full((NCTX, KV, HD)), full((NCTX, SL, HD))],
        compiler_params=params(),
        cost_estimate=cost(1 << 20, 1 << 21),
    )(received, *after)


def local_kernel(x_ref, b_ref, c_ref, d_ref, o_ref):
    cum = row_cumulative(d_ref[...])
    cum_col = col_cumulative(d_ref[...])
    cross = lax.dot_general(
        c_ref[...], b_ref[...], (((1,), (1,)), ((), ())), preferred_element_type=F32
    )
    mask = tri(True)
    for h in range(MH):
        gap = jnp.where(mask, cum_col[:, h : h + 1] - cum[h : h + 1, :], -1e30)
        w = (jnp.exp(gap) * cross).astype(BF16)
        o_ref[:, h * HD : (h + 1) * HD] = jnp.dot(
            w, x_ref[:, h * HD : (h + 1) * HD], preferred_element_type=F32
        )


def local_part(x_in, b_in, c_in, decay_log):
    return pl.pallas_call(
        local_kernel,
        out_shape=jax.ShapeDtypeStruct((L, MH * HD), F32),
        in_specs=[VM] * 4,
        out_specs=VM,
        compiler_params=params(LARGE),
        cost_estimate=cost(1 << 28, 1 << 21),
    )(x_in, b_in, c_in, decay_log)


JOIN_COST = 1 << 26


def join_kernel(l_ref, e_ref, c_ref, d_ref, o_ref):
    grow = jnp.exp(col_cumulative(d_ref[...]))
    c = c_ref[...]
    for h in range(MH):
        cols = slice(h * HD, (h + 1) * HD)
        readout = jnp.dot(c, e_ref[cols, :], preferred_element_type=F32)
        o_ref[:, cols] = (l_ref[:, cols] + grow[:, h : h + 1] * readout).astype(BF16)


def join_mamba(local, entering, c_in, decay_log):
    return pl.pallas_call(
        join_kernel,
        out_shape=jax.ShapeDtypeStruct((L, MH * HD), BF16),
        in_specs=[VM] * 4,
        out_specs=VM,
        compiler_params=params(LARGE),
        cost_estimate=cost(JOIN_COST, 1 << 21),
    )(local, entering, c_in, decay_log)


ROWS = QH * L
SCALE2 = LOG2E / math.sqrt(HD)


def stacked_queries(q_ref):
    return jnp.concatenate([q_ref[:, g * HD : (g + 1) * HD] for g in range(QH)], axis=0)


def accumulate(state, s, v):
    m_old, total, acc = state
    m = jnp.maximum(m_old, jnp.max(s, axis=1, keepdims=True))
    factor = jnp.exp2((m_old - m) * SCALE2)
    p = jnp.exp2((s - m) * SCALE2)
    part = p[:, :L]
    for j in range(1, p.shape[1] // L):
        part = part + p[:, j * L : (j + 1) * L]
    added = jnp.dot(p.astype(BF16), v, preferred_element_type=F32)
    return m, total * factor + part, acc * factor + added


def scores(q, k):
    return lax.dot_general(q, k, (((1,), (1,)), ((), ())), preferred_element_type=F32)


def open_kernel(q_ref, q2_ref, k_ref, v_ref, s_ref, s2_ref, m_ref, l_ref, a_ref):
    q = stacked_queries(q_ref)
    s_ref[...] = q
    s2_ref[...] = stacked_queries(q2_ref)
    s = scores(q, k_ref[...])
    t = lax.broadcasted_iota(jnp.int32, s.shape, 0) % L
    u = lax.broadcasted_iota(jnp.int32, s.shape, 1)
    s = jnp.where(u <= t, s, -1e30)
    m = jnp.max(s, axis=1, keepdims=True)
    p = jnp.exp2((s - m) * SCALE2)
    m_ref[...] = jnp.broadcast_to(m, (ROWS, L))
    l_ref[...] = p
    a_ref[...] = jnp.dot(p.astype(BF16), v_ref[...], preferred_element_type=F32)


PART = jax.ShapeDtypeStruct((ROWS, L), F32)


def open_attention(q_in, q_other, k_in, v_in):
    return pl.pallas_call(
        open_kernel,
        out_shape=[jax.ShapeDtypeStruct((ROWS, HD), BF16)] * 2 + [PART] * 3,
        in_specs=[VM] * 4,
        out_specs=[VM] * 5,
        compiler_params=params(LARGE),
        cost_estimate=cost(1 << 27, 1 << 20),
    )(q_in, q_other, k_in, v_in)


def attend_kernel(n_sets, n_ties, fresh, pack, other, me_ref, q_ref, *refs):
    if not fresh:
        m_in, l_in, a_in = refs[:3]
        refs = refs[3:]
    sets, refs = refs[:n_sets], refs[n_sets + n_ties :]
    if pack:
        o_ref, m_ref, l_ref, a_ref = refs
    else:
        m_ref, l_ref, a_ref = refs
    me = (me_ref[0] ^ 1) if other else me_ref[0]
    q = q_ref[...]
    if fresh:
        m_ref[...] = jnp.full((ROWS, L), -1e30, F32)
        l_ref[...] = jnp.zeros((ROWS, L), F32)
        a_ref[...] = jnp.zeros((ROWS, HD), F32)
    else:
        m_ref[...] = m_in[...]
        l_ref[...] = l_in[...]
        a_ref[...] = a_in[...]
    keys = NCTX * PIECE
    shard = lax.broadcasted_iota(jnp.int32, (1, keys), 1) // PIECE
    bias = jnp.where(shard < me, 0.0, -1e30)

    @pl.when(me > 0)
    def _():
        for ref in sets:
            k = ref[:, 0:PIECE, :].reshape(keys, HD)
            v = ref[:, PIECE:KV, :].reshape(keys, HD)
            s = scores(q, k) + bias
            m, total, acc = accumulate((m_ref[:, :1], l_ref[...], a_ref[...]), s, v)
            m_ref[...] = jnp.broadcast_to(m, (ROWS, L))
            l_ref[...] = total
            a_ref[...] = acc

    if pack:
        lane = lax.broadcasted_iota(jnp.int32, (ROWS, L), 1)
        total = jnp.sum(l_ref[...], axis=1, keepdims=True)
        o_ref[:, :HD] = a_ref[...]
        o_ref[:, HD:] = jnp.where(lane < L // 2, m_ref[...], total)


def attend(me, queries, carry, sets, other=False, pack=False, after=()):
    def kernel(*refs):
        attend_kernel(len(sets), len(after), not carry, pack, other, *refs)

    return pl.pallas_call(
        kernel,
        grid=(1,),
        out_shape=jax.ShapeDtypeStruct((ROWS, HD + L), F32) if pack else [PART] * 3,
        in_specs=[SM, full(queries.shape)]
        + [full(PART.shape)] * len(carry)
        + [full(s.shape) for s in sets]
        + [TILE] * len(after),
        out_specs=full((ROWS, HD + L)) if pack else [full(PART.shape)] * 3,
        scratch_shapes=[pltpu.VMEM((ROWS, L), F32)] * 3 if pack else [],
        compiler_params=params(),
        cost_estimate=cost(1 << 28, len(sets) << 20),
    )(me, queries, *carry, *sets, *after)


def merge_kernel(m_ref, l_ref, a_ref, p_ref, o_ref):
    m1, m2 = m_ref[:, :1], p_ref[:, HD : HD + 1]
    m = jnp.maximum(m1, m2)
    f1, f2 = jnp.exp2((m1 - m) * SCALE2), jnp.exp2((m2 - m) * SCALE2)
    total = jnp.sum(l_ref[...], axis=1, keepdims=True) * f1 + p_ref[:, HD + L - 1 :] * f2
    out = (a_ref[...] * f1 + p_ref[:, :HD] * f2) / total
    for g in range(QH):
        o_ref[:, g * HD : (g + 1) * HD] = out[g * L : (g + 1) * L].astype(BF16)


def merge_attention(carry, part):
    return pl.pallas_call(
        merge_kernel,
        out_shape=jax.ShapeDtypeStruct((L, QH * HD), BF16),
        in_specs=[VM] * 4,
        out_specs=VM,
        compiler_params=params(),
        cost_estimate=cost(1 << 20, 1 << 20),
    )(*carry, part)


CHIPS_X = 4


def along_x(step):
    pairs = []
    for i in range(NCTX):
        y, x, c = i // (2 * CHIPS_X), i // 2 % CHIPS_X, i % 2
        pairs.append((i, (y * CHIPS_X + (x + step) % CHIPS_X) * 2 + c))
    return pairs


def other_core(value):
    return lax.ppermute(value, "ctx", [(i, i ^ 1) for i in range(NCTX)])


def context_parts(x_in, b_in, c_in, decay_log, q_in, k_in, v_in, expert_out):
    me = lax.axis_index("ctx").astype(jnp.int32).reshape(1)
    chunks = chunks_to_send(x_in, b_in, decay_log, k_in, v_in)
    received = lax.all_to_all(chunks, "ctx", split_axis=0, concat_axis=0, tiled=True)
    q_other = other_core(q_in)
    q_own, q_other, *carry = open_attention(q_in, q_other, k_in, v_in)
    local = local_part(x_in, b_in, c_in, decay_log)
    sent = chunks.reshape(NCTX * CHUNK, HD)
    blocks = expert_blocks(expert_out, [sent, local, q_own])
    nearer = [blocks[d] for d in (1, 7, 2, 6, 3, 5) if d < len(blocks)]
    own, opposite, entering = take_received(received, nearer)
    right = lax.ppermute(own, "ctx", along_x(1))
    left = lax.ppermute(own, "ctx", along_x(-1))

    entering = lax.all_to_all(entering, "ctx", split_axis=0, concat_axis=0, tiled=True)
    mamba_out = join_mamba(local, entering.reshape(MH * L, HD), c_in, decay_log)

    carry = attend(me, q_own, carry, [own, opposite])
    carry_other = attend(me, q_other, [], [own, opposite], other=True)
    farthest = blocks[4:5]
    part = attend(
        me, q_other, carry_other, [right, left], other=True, pack=True, after=[*farthest, carry[0]]
    )
    part = other_core(part)
    carry = attend(me, q_own, carry, [right, left])
    return mamba_out, merge_attention(carry, part), blocks


def blocks_kernel(n_ties, me_ref, e_ref, *refs):
    outs = refs[n_ties:]
    for d, o_ref in enumerate(outs):
        to = lax.rem(me_ref[0] + d, len(outs))
        o_ref[...] = jnp.concatenate(
            [e_ref[0, i, to].astype(F32) for i in range(e_ref.shape[1])], axis=0
        ).astype(BF16)


def combine_kernel(me_ref, ids_ref, idst_ref, gates_ref, *refs):
    rows_refs, o_ref = refs[:-1], refs[-1]
    peers = len(rows_refs)
    rows = jnp.concatenate([r[...].astype(F32) for r in rows_refs], axis=0).astype(BF16)
    owned = rows.shape[0] // (peers * CAP)
    count = ids_ref.shape[0]
    ids, idst, gates = ids_ref[...], idst_ref[...], gates_ref[...]
    t = lax.broadcasted_iota(jnp.int32, (count, count), 0)
    u = lax.broadcasted_iota(jnp.int32, (count, count), 1)
    place = lax.broadcasted_iota(jnp.int32, (count, rows.shape[0]), 1)
    out = None
    for k in range(2):
        mine = ids[:, k : k + 1]
        slot = jnp.zeros((count, 1), jnp.int32)
        for j in range(2):
            before = (u < t) if j >= k else (u <= t)
            same = jnp.logical_and(before, idst[j : j + 1, :] == mine)
            slot = slot + jnp.sum(same.astype(jnp.int32), axis=1, keepdims=True)
        distance = (me_ref[0] - mine // owned + peers) % peers
        number = (distance * owned + mine % owned) * CAP + slot
        pick = (place == number).astype(F32).astype(BF16)
        row = jnp.dot(pick, rows, preferred_element_type=F32)
        term = gates[:, k : k + 1] * row
        out = term if out is None else out + term
    o_ref[...] = out.astype(BF16)


def expert_blocks(expert_out, after):
    owned, peers, cap, width = expert_out.shape[1:]
    me = lax.axis_index("grp").astype(jnp.int32).reshape(1)
    def kernel(*refs):
        blocks_kernel(len(after), *refs)

    held = pl.pallas_call(
        kernel,
        out_shape=[jax.ShapeDtypeStruct((owned * cap, width), BF16)] * peers,
        grid=(1,),
        in_specs=[SM, full(expert_out.shape)] + [TILE] * len(after),
        out_specs=[full((owned * cap, width))] * peers,
        compiler_params=params(LARGE),
        cost_estimate=cost(1 << 20, 1 << 21),
    )(me, expert_out, *after)
    blocks = list(held)
    for d in sorted(range(1, peers), key=lambda d: min(d, peers - d)):
        pairs = [(i, (i + d) % peers) for i in range(peers)]
        blocks[d] = lax.ppermute(held[d], "grp", pairs)
    return blocks


def expert_part(expert_ids, gates, blocks):
    me = lax.axis_index("grp").astype(jnp.int32).reshape(1)
    peers = len(blocks)
    rows, width = blocks[0].shape
    count = expert_ids.shape[0]
    block = 2048
    return pl.pallas_call(
        combine_kernel,
        grid=(width // block,),
        out_shape=jax.ShapeDtypeStruct((count, width), BF16),
        in_specs=[
            SM,
            pl.BlockSpec((count, 2), lambda i: (0, 0)),
            pl.BlockSpec((2, count), lambda i: (0, 0)),
            pl.BlockSpec((count, 2), lambda i: (0, 0)),
        ]
        + [pl.BlockSpec((rows, block), lambda i: (0, i))] * peers,
        out_specs=pl.BlockSpec((count, block), lambda i: (0, i)),
        compiler_params=params(LARGE),
        cost_estimate=cost(1 << 24, 1 << 20),
    )(me, expert_ids, expert_ids.T, gates, *blocks)


def shards(x_in, b_in, c_in, decay_log, q_in, k_in, v_in, expert_ids, gates, expert_out):
    mamba_out, attn_out, blocks = context_parts(
        x_in, b_in, c_in, decay_log, q_in, k_in, v_in, expert_out
    )
    moe_out = expert_part(expert_ids, gates, blocks)
    return (mamba_out, attn_out, moe_out)


def solution(mesh):
    return jax.shard_map(
        shards,
        mesh=mesh,
        in_specs=(
            P("ctx", "grp"),
            P("ctx", None),
            P("ctx", None),
            P("grp", "ctx"),
            P("ctx", "grp"),
            P("ctx", "grp"),
            P("ctx", "grp"),
            P(("ctx", "grp"), None),
            P(("ctx", "grp"), None),
            P("ctx", "grp", None, None, None),
        ),
        out_specs=(P("ctx", "grp"), P("ctx", "grp"), P(("ctx", "grp"), None)),
        check_vma=False,
    )
```

```python
import math

import jax
import jax.numpy as jnp
from jax import lax
from jax.experimental import pallas as pl
from jax.experimental.pallas import tpu as pltpu
from jax.sharding import PartitionSpec as P

HD = 128
L = 128
MH = 16
NCTX = 64
QH = 4
CAP = 4
LOG2E = 1.4426950408889634
F32 = jnp.float32
BF16 = jnp.bfloat16
VM = pl.BlockSpec(memory_space=pltpu.VMEM)
SM = pl.BlockSpec(memory_space=pltpu.SMEM)
TILE = pl.BlockSpec((8, 128), lambda i: (0, 0))


GRANT = 62


def params(mib=GRANT):
    return pltpu.CompilerParams(vmem_limit_bytes=mib * 2**20)


def full(shape):
    return pl.BlockSpec(shape, lambda i: (0,) * len(shape))


def cost(flops, nbytes):
    return pl.CostEstimate(flops=flops, bytes_accessed=nbytes, transcendentals=0)


def tri(lower):
    r = lax.broadcasted_iota(jnp.int32, (L, L), 0)
    c = lax.broadcasted_iota(jnp.int32, (L, L), 1)
    return (c <= r) if lower else (r <= c)


def row_cumulative(decay):
    return jnp.dot(
        decay, tri(False).astype(F32), precision=lax.Precision.HIGHEST, preferred_element_type=F32
    )


def col_cumulative(decay):
    return lax.dot_general(
        tri(True).astype(F32),
        decay,
        (((1,), (1,)), ((), ())),
        precision=lax.Precision.HIGHEST,
        preferred_element_type=F32,
    )


PIECE = 16
KV = 2 * PIECE
SL = 32
CHUNK = 2 * KV + SL + 8


def send_kernel(x_ref, b_ref, d_ref, k_ref, v_ref, o_ref):
    cum = row_cumulative(d_ref[...])
    tail = jnp.exp(cum[:, L - 1 :] - cum)
    block_decay = jnp.exp(cum[:, L - 1 :])
    bt = b_ref[...].astype(F32).T
    row = lax.broadcasted_iota(jnp.int32, (8, L), 0)
    pieces = L // PIECE
    for h in range(MH):
        wb = (tail[h : h + 1, :] * bt).astype(BF16)
        s = jnp.dot(wb, x_ref[:, h * HD : (h + 1) * HD], preferred_element_type=F32)
        d = jnp.broadcast_to(block_decay[h : h + 1, :], (8, L))
        hi = d.astype(BF16).astype(F32)
        mid = (d - hi).astype(BF16).astype(F32)
        lo = d - hi - mid
        terms = jnp.where(row == 0, hi, jnp.where(row == 1, mid, jnp.where(row == 2, lo, 0.0)))
        for q in range(4):
            j = h * 4 + q
            for turn in range(2):
                at = (j + turn * pieces // 2) % pieces * PIECE
                o_ref[j, turn * KV : turn * KV + PIECE, :] = k_ref[at : at + PIECE, :]
                o_ref[j, turn * KV + PIECE : (turn + 1) * KV, :] = v_ref[at : at + PIECE, :]
            o_ref[j, 2 * KV : CHUNK, :] = jnp.concatenate(
                [s[q * SL : (q + 1) * SL], terms], axis=0
            ).astype(BF16)


def chunks_to_send(x_in, b_in, decay_log, k_in, v_in):
    return pl.pallas_call(
        send_kernel,
        out_shape=jax.ShapeDtypeStruct((NCTX, CHUNK, HD), BF16),
        in_specs=[VM] * 5,
        out_specs=VM,
        compiler_params=params(),
        cost_estimate=cost(1 << 26, 1 << 21),
    )(x_in, b_in, decay_log, k_in, v_in)


def take_kernel(s_ref, *refs):
    own_ref, opposite_ref = refs[-2:]
    own_ref[...] = s_ref[:, :KV, :]
    opposite_ref[...] = s_ref[:, KV : 2 * KV, :]


def take_received(received, after):
    piece = (NCTX, KV, HD)
    return pl.pallas_call(
        take_kernel,
        grid=(1,),
        out_shape=[jax.ShapeDtypeStruct(piece, BF16)] * 2,
        in_specs=[pl.BlockSpec((NCTX, 2 * KV, HD), lambda i: (0, 0, 0))] + [TILE] * len(after),
        out_specs=[full(piece)] * 2,
        compiler_params=params(),
        cost_estimate=cost(1 << 20, 1 << 21),
    )(received, *after)


def scan_kernel(s_ref, *refs):
    o_ref = refs[-1]

    def step(k, e):
        o_ref[k] = e.astype(BF16)
        block = s_ref[k, 2 * KV : CHUNK, :].astype(F32)
        d = block[SL : SL + 1] + block[SL + 1 : SL + 2] + block[SL + 2 : SL + 3]
        return d * e + block[:SL]

    lax.fori_loop(0, NCTX, step, jnp.zeros((SL, HD), F32), unroll=8)


def scan_states(received, after):
    return pl.pallas_call(
        scan_kernel,
        grid=(1,),
        out_shape=jax.ShapeDtypeStruct((NCTX, SL, HD), BF16),
        in_specs=[full(received.shape)] + [TILE] * len(after),
        out_specs=full((NCTX, SL, HD)),
        compiler_params=params(),
        cost_estimate=cost(1 << 20, 1 << 21),
    )(received, *after)


def local_kernel(x_ref, b_ref, c_ref, d_ref, o_ref, token_ref):
    token_ref[...] = jnp.zeros((8, HD), F32)
    cum = row_cumulative(d_ref[...])
    cum_col = col_cumulative(d_ref[...])
    cross = lax.dot_general(
        c_ref[...], b_ref[...], (((1,), (1,)), ((), ())), preferred_element_type=F32
    )
    mask = tri(True)
    for h in range(MH):
        gap = jnp.where(mask, cum_col[:, h : h + 1] - cum[h : h + 1, :], -1e30)
        w = (jnp.exp(gap) * cross).astype(BF16)
        o_ref[:, h * HD : (h + 1) * HD] = jnp.dot(
            w, x_ref[:, h * HD : (h + 1) * HD], preferred_element_type=F32
        )


TOKEN = jax.ShapeDtypeStruct((8, HD), F32)


def local_part(x_in, b_in, c_in, decay_log):
    return pl.pallas_call(
        local_kernel,
        out_shape=[jax.ShapeDtypeStruct((L, MH * HD), F32), TOKEN],
        in_specs=[VM] * 4,
        out_specs=[VM] * 2,
        compiler_params=params(),
        cost_estimate=cost(1 << 28, 1 << 21),
    )(x_in, b_in, c_in, decay_log)


JOIN_COST = 1 << 26


JOIN_HEADS = 4


def join_kernel(l_ref, e_ref, c_ref, d_ref, o_ref):
    cum = col_cumulative(d_ref[...])
    head = lax.broadcasted_iota(jnp.int32, cum.shape, 1)
    c = c_ref[...]
    for i in range(JOIN_HEADS):
        h = pl.program_id(0) * JOIN_HEADS + i
        grow = jnp.exp(jnp.sum(jnp.where(head == h, cum, 0.0), axis=1, keepdims=True))
        cols = slice(i * HD, (i + 1) * HD)
        readout = jnp.dot(c, e_ref[cols, :], preferred_element_type=F32)
        o_ref[:, cols] = (l_ref[:, cols] + grow * readout).astype(BF16)


def join_mamba(local, entering, c_in, decay_log):
    wide = JOIN_HEADS * HD
    return pl.pallas_call(
        join_kernel,
        grid=(MH // JOIN_HEADS,),
        out_shape=jax.ShapeDtypeStruct((L, MH * HD), BF16),
        in_specs=[
            pl.BlockSpec((L, wide), lambda i: (0, i)),
            pl.BlockSpec((wide, HD), lambda i: (i, 0)),
            full(c_in.shape),
            full(decay_log.shape),
        ],
        out_specs=pl.BlockSpec((L, wide), lambda i: (0, i)),
        compiler_params=params(),
        cost_estimate=cost(JOIN_COST, 1 << 21),
    )(local, entering, c_in, decay_log)


ROWS = QH * L
SCALE2 = LOG2E / math.sqrt(HD)


def stacked_queries(q_ref):
    return jnp.concatenate([q_ref[:, g * HD : (g + 1) * HD] for g in range(QH)], axis=0)


def accumulate(state, s, v):
    m_old, total, acc = state
    m = jnp.maximum(m_old, jnp.max(s, axis=1, keepdims=True))
    factor = jnp.exp2((m_old - m) * SCALE2)
    p = jnp.exp2((s - m) * SCALE2)
    part = p[:, :L]
    for j in range(1, p.shape[1] // L):
        part = part + p[:, j * L : (j + 1) * L]
    added = jnp.dot(p.astype(BF16), v, preferred_element_type=F32)
    return m, total * factor + part, acc * factor + added


def scores(q, k):
    return lax.dot_general(q, k, (((1,), (1,)), ((), ())), preferred_element_type=F32)


def packed(m, total):
    lane = lax.broadcasted_iota(jnp.int32, (ROWS, L), 1)
    return jnp.where(lane < L // 2, m, jnp.sum(total, axis=1, keepdims=True))


def unpacked(ref, at=0):
    lane = lax.broadcasted_iota(jnp.int32, (ROWS, L), 1)
    return ref[:, at : at + 1], jnp.where(lane == 0, ref[:, at + L - 1 : at + L], 0.0)


def open_kernel(q_ref, q2_ref, k_ref, v_ref, _, s_ref, s2_ref, ml_ref, a_ref, token_ref):
    token_ref[...] = jnp.zeros((8, HD), F32)
    q = stacked_queries(q_ref)
    s_ref[...] = q
    s2_ref[...] = stacked_queries(q2_ref)
    s = scores(q, k_ref[...])
    t = lax.broadcasted_iota(jnp.int32, s.shape, 0) % L
    u = lax.broadcasted_iota(jnp.int32, s.shape, 1)
    s = jnp.where(u <= t, s, -1e30)
    m = jnp.max(s, axis=1, keepdims=True)
    p = jnp.exp2((s - m) * SCALE2)
    ml_ref[...] = packed(m, p)
    a_ref[...] = jnp.dot(p.astype(BF16), v_ref[...], preferred_element_type=F32)


PART = jax.ShapeDtypeStruct((ROWS, L), F32)


def open_attention(q_in, q_other, k_in, v_in, after):
    return pl.pallas_call(
        open_kernel,
        out_shape=[jax.ShapeDtypeStruct((ROWS, HD), BF16)] * 2 + [PART] * 2 + [TOKEN],
        in_specs=[VM] * 5,
        out_specs=[VM] * 5,
        compiler_params=params(),
        cost_estimate=cost(1 << 27, 1 << 20),
    )(q_in, q_other, k_in, v_in, after)


def go_on(me, q, state, sets):
    keys = NCTX * PIECE
    shard = lax.broadcasted_iota(jnp.int32, (1, keys), 1) // PIECE
    bias = jnp.where(shard < me, 0.0, -1e30)
    for ref in sets:
        k = ref[:, 0:PIECE, :].reshape(keys, HD)
        v = ref[:, PIECE:KV, :].reshape(keys, HD)
        state = accumulate(state, scores(q, k) + bias, v)
    return state


def early_kernel(me_ref, q_ref, q2_ref, ml_ref, a_ref, *refs):
    sets, (ml1_ref, a1_ref, ml2_ref, a2_ref) = refs[:2], refs[2:]
    me = me_ref[0]
    m, total, acc = go_on(me, q_ref[...], (*unpacked(ml_ref), a_ref[...]), sets)
    ml1_ref[...] = packed(m, total)
    a1_ref[...] = acc
    none = jnp.full((ROWS, 1), -1e30, F32), jnp.zeros((ROWS, L), F32), jnp.zeros((ROWS, HD), F32)
    m, total, acc = go_on(me ^ 1, q2_ref[...], none, sets)
    ml2_ref[...] = packed(m, total)
    a2_ref[...] = acc


def early_attention(me, q_own, q_other, ml, acc, sets):
    return pl.pallas_call(
        early_kernel,
        out_shape=[PART] * 4,
        in_specs=[SM] + [VM] * 6,
        out_specs=[VM] * 4,
        compiler_params=params(),
        cost_estimate=cost(1 << 29, 1 << 22),
    )(me, q_own, q_other, ml, acc, *sets)


def other_kernel(me_ref, q_ref, ml_ref, a_ref, r_ref, l_ref, o_ref):
    state = (*unpacked(ml_ref), a_ref[...])
    m, total, acc = go_on(me_ref[0] ^ 1, q_ref[...], state, (r_ref, l_ref))
    o_ref[:, :HD] = acc
    o_ref[:, HD:] = packed(m, total)


def own_kernel(me_ref, q_ref, ml_ref, a_ref, r_ref, l_ref, mlo_ref, ao_ref):
    state = (*unpacked(ml_ref), a_ref[...])
    m, total, acc = go_on(me_ref[0], q_ref[...], state, (r_ref, l_ref))
    mlo_ref[...] = packed(m, total)
    ao_ref[...] = acc


def late_attention(kernel, outs, me, queries, ml, acc, sets):
    return pl.pallas_call(
        kernel,
        out_shape=outs,
        in_specs=[SM] + [VM] * 5,
        out_specs=[VM] * len(outs),
        compiler_params=params(),
        cost_estimate=cost(1 << 28, 1 << 21),
    )(me, queries, ml, acc, *sets)


def merge_kernel(ml_ref, a_ref, p_ref, o_ref):
    m1, m2 = ml_ref[:, :1], p_ref[:, HD : HD + 1]
    m = jnp.maximum(m1, m2)
    f1, f2 = jnp.exp2((m1 - m) * SCALE2), jnp.exp2((m2 - m) * SCALE2)
    total = ml_ref[:, L - 1 :] * f1 + p_ref[:, HD + L - 1 :] * f2
    out = (a_ref[...] * f1 + p_ref[:, :HD] * f2) / total
    for g in range(QH):
        o_ref[:, g * HD : (g + 1) * HD] = out[g * L : (g + 1) * L].astype(BF16)


def merge_attention(ml, acc, part):
    return pl.pallas_call(
        merge_kernel,
        out_shape=jax.ShapeDtypeStruct((L, QH * HD), BF16),
        in_specs=[VM] * 3,
        out_specs=VM,
        compiler_params=params(),
        cost_estimate=cost(1 << 20, 1 << 20),
    )(ml, acc, part)


CHIPS_X = 4


def along_x(step):
    pairs = []
    for i in range(NCTX):
        y, x, c = i // (2 * CHIPS_X), i // 2 % CHIPS_X, i % 2
        pairs.append((i, (y * CHIPS_X + (x + step) % CHIPS_X) * 2 + c))
    return pairs


def other_core(value):
    return lax.ppermute(value, "ctx", [(i, i ^ 1) for i in range(NCTX)])


def context_parts(x_in, b_in, c_in, decay_log, q_in, k_in, v_in, expert_out):
    me = lax.axis_index("ctx").astype(jnp.int32).reshape(1)
    chunks = chunks_to_send(x_in, b_in, decay_log, k_in, v_in)
    received = lax.all_to_all(chunks, "ctx", split_axis=0, concat_axis=0, tiled=True)
    q_other = other_core(q_in)
    local, token = local_part(x_in, b_in, c_in, decay_log)
    q_own, q_other, ml, acc, token = open_attention(q_in, q_other, k_in, v_in, token)
    blocks = expert_blocks(expert_out, [chunks.reshape(NCTX * CHUNK, HD)])
    own, opposite = take_received(received, [token, *blocks[1:]])
    right = lax.ppermute(own, "ctx", along_x(1))
    left = lax.ppermute(own, "ctx", along_x(-1))

    ml, acc, ml2, acc2 = early_attention(me, q_own, q_other, ml, acc, [own, opposite])
    entering = scan_states(received, [ml2])
    entering = lax.all_to_all(entering, "ctx", split_axis=0, concat_axis=0, tiled=True)
    mamba_out = join_mamba(local, entering.reshape(MH * L, HD), c_in, decay_log)

    sets = [right, left]
    both = jax.ShapeDtypeStruct((ROWS, HD + L), F32)
    [part] = late_attention(other_kernel, [both], me, q_other, ml2, acc2, sets)
    part = other_core(part)
    ml, acc = late_attention(own_kernel, [PART] * 2, me, q_own, ml, acc, sets)
    return mamba_out, merge_attention(ml, acc, part), blocks


def blocks_kernel(n_ties, me_ref, e_ref, *refs):
    outs = refs[n_ties:]
    for d, o_ref in enumerate(outs):
        to = lax.rem(me_ref[0] + d, len(outs))
        o_ref[...] = jnp.concatenate(
            [e_ref[0, i, to].astype(F32) for i in range(e_ref.shape[1])], axis=0
        ).astype(BF16)


def combine_kernel(me_ref, idst_ref, gatest_ref, *refs):
    rows_refs, o_ref = refs[:-1], refs[-1]
    peers = len(rows_refs)
    rows = jnp.concatenate([r[...].astype(F32) for r in rows_refs], axis=0).astype(BF16)
    owned = rows.shape[0] // (peers * CAP)
    count = idst_ref.shape[1]
    idst, gatest = idst_ref[...], gatest_ref[...]
    t = lax.broadcasted_iota(jnp.int32, (count, count), 0)
    u = lax.broadcasted_iota(jnp.int32, (count, count), 1)
    place = lax.broadcasted_iota(jnp.int32, (count, rows.shape[0]), 1)

    def column(row):
        return jnp.sum(jnp.where(t == u, row, jnp.zeros_like(row)), axis=1, keepdims=True)

    out = None
    for k in range(2):
        mine = column(idst[k : k + 1, :])
        slot = jnp.zeros((count, 1), jnp.int32)
        for j in range(2):
            before = (u < t) if j >= k else (u <= t)
            same = jnp.logical_and(before, idst[j : j + 1, :] == mine)
            slot = slot + jnp.sum(same.astype(jnp.int32), axis=1, keepdims=True)
        distance = (me_ref[0] - mine // owned + peers) % peers
        number = (distance * owned + mine % owned) * CAP + slot
        pick = (place == number).astype(F32).astype(BF16)
        row = jnp.dot(pick, rows, preferred_element_type=F32)
        term = column(gatest[k : k + 1, :]) * row
        out = term if out is None else out + term
    o_ref[...] = out.astype(BF16)


def expert_blocks(expert_out, after):
    owned, peers, cap, width = expert_out.shape[1:]
    me = lax.axis_index("grp").astype(jnp.int32).reshape(1)
    def kernel(*refs):
        blocks_kernel(len(after), *refs)

    held = pl.pallas_call(
        kernel,
        out_shape=[jax.ShapeDtypeStruct((owned * cap, width), BF16)] * peers,
        grid=(1,),
        in_specs=[SM, full(expert_out.shape)] + [TILE] * len(after),
        out_specs=[full((owned * cap, width))] * peers,
        compiler_params=params(),
        cost_estimate=cost(1 << 20, 1 << 21),
    )(me, expert_out, *after)
    blocks = list(held)
    for d in sorted(range(1, peers), key=lambda d: (1, 7, 2, 6, 4, 3, 5).index(d)):
        pairs = [(i, (i + d) % peers) for i in range(peers)]
        blocks[d] = lax.ppermute(held[d], "grp", pairs)
    return blocks


def expert_part(expert_ids, gates, blocks):
    me = lax.axis_index("grp").astype(jnp.int32).reshape(1)
    peers = len(blocks)
    rows, width = blocks[0].shape
    count = expert_ids.shape[0]
    return pl.pallas_call(
        combine_kernel,
        grid=(1,),
        out_shape=jax.ShapeDtypeStruct((count, width), BF16),
        in_specs=[SM, full((2, count)), full((2, count))] + [full((rows, width))] * peers,
        out_specs=full((count, width)),
        compiler_params=params(),
        cost_estimate=cost(1 << 24, 1 << 20),
    )(me, expert_ids.T, gates.T, *blocks)


def shards(x_in, b_in, c_in, decay_log, q_in, k_in, v_in, expert_ids, gates, expert_out):
    mamba_out, attn_out, blocks = context_parts(
        x_in, b_in, c_in, decay_log, q_in, k_in, v_in, expert_out
    )
    moe_out = expert_part(expert_ids, gates, blocks)
    return (mamba_out, attn_out, moe_out)


def solution(mesh):
    return jax.shard_map(
        shards,
        mesh=mesh,
        in_specs=(
            P("ctx", "grp"),
            P("ctx", None),
            P("ctx", None),
            P("grp", "ctx"),
            P("ctx", "grp"),
            P("ctx", "grp"),
            P("ctx", "grp"),
            P(("ctx", "grp"), None),
            P(("ctx", "grp"), None),
            P("ctx", "grp", None, None, None),
        ),
        out_specs=(P("ctx", "grp"), P("ctx", "grp"), P(("ctx", "grp"), None)),
        check_vma=False,
    )
```

```python
import math

import jax
import jax.numpy as jnp
from jax import lax
from jax.experimental import pallas as pl
from jax.experimental.pallas import tpu as pltpu
from jax.sharding import PartitionSpec as P

HD = 128
L = 128
MH = 16
NCTX = 64
QH = 4
CAP = 4
LOG2E = 1.4426950408889634
F32 = jnp.float32
BF16 = jnp.bfloat16
VM = pl.BlockSpec(memory_space=pltpu.VMEM)
SM = pl.BlockSpec(memory_space=pltpu.SMEM)
TILE = pl.BlockSpec((8, 128), lambda i: (0, 0))


LARGE, SMALL = 60, 24


def params(mib=SMALL):
    return pltpu.CompilerParams(vmem_limit_bytes=mib * 2**20)


def full(shape):
    return pl.BlockSpec(shape, lambda i: (0,) * len(shape))


def cost(flops, nbytes):
    return pl.CostEstimate(flops=flops, bytes_accessed=nbytes, transcendentals=0)


def tri(lower):
    r = lax.broadcasted_iota(jnp.int32, (L, L), 0)
    c = lax.broadcasted_iota(jnp.int32, (L, L), 1)
    return (c <= r) if lower else (r <= c)


def row_cumulative(decay):
    return jnp.dot(
        decay, tri(False).astype(F32), precision=lax.Precision.HIGHEST, preferred_element_type=F32
    )


def col_cumulative(decay):
    return lax.dot_general(
        tri(True).astype(F32),
        decay,
        (((1,), (1,)), ((), ())),
        precision=lax.Precision.HIGHEST,
        preferred_element_type=F32,
    )


PIECE = 16
KV = 2 * PIECE
SL = 32
CHUNK = 2 * KV + SL + 8


def send_kernel(x_ref, b_ref, d_ref, k_ref, v_ref, o_ref):
    cum = row_cumulative(d_ref[...])
    tail = jnp.exp(cum[:, L - 1 :] - cum)
    block_decay = jnp.exp(cum[:, L - 1 :])
    bt = b_ref[...].astype(F32).T
    row = lax.broadcasted_iota(jnp.int32, (8, L), 0)
    pieces = L // PIECE
    for h in range(MH):
        wb = (tail[h : h + 1, :] * bt).astype(BF16)
        s = jnp.dot(wb, x_ref[:, h * HD : (h + 1) * HD], preferred_element_type=F32)
        d = jnp.broadcast_to(block_decay[h : h + 1, :], (8, L))
        hi = d.astype(BF16).astype(F32)
        mid = (d - hi).astype(BF16).astype(F32)
        lo = d - hi - mid
        terms = jnp.where(row == 0, hi, jnp.where(row == 1, mid, jnp.where(row == 2, lo, 0.0)))
        for q in range(4):
            j = h * 4 + q
            for turn in range(2):
                at = (j + turn * pieces // 2) % pieces * PIECE
                o_ref[j, turn * KV : turn * KV + PIECE, :] = k_ref[at : at + PIECE, :]
                o_ref[j, turn * KV + PIECE : (turn + 1) * KV, :] = v_ref[at : at + PIECE, :]
            o_ref[j, 2 * KV : CHUNK, :] = jnp.concatenate(
                [s[q * SL : (q + 1) * SL], terms], axis=0
            ).astype(BF16)


def chunks_to_send(x_in, b_in, decay_log, k_in, v_in):
    return pl.pallas_call(
        send_kernel,
        out_shape=jax.ShapeDtypeStruct((NCTX, CHUNK, HD), BF16),
        in_specs=[VM] * 5,
        out_specs=VM,
        compiler_params=params(LARGE),
        cost_estimate=cost(1 << 26, 1 << 21),
    )(x_in, b_in, decay_log, k_in, v_in)


def take_kernel(s_ref, *refs):
    own_ref, opposite_ref, o_ref = refs[-3:]
    own_ref[...] = s_ref[:, :KV, :]
    opposite_ref[...] = s_ref[:, KV : 2 * KV, :]

    def step(k, e):
        o_ref[k] = e.astype(BF16)
        block = s_ref[k, 2 * KV : CHUNK, :].astype(F32)
        d = block[SL : SL + 1] + block[SL + 1 : SL + 2] + block[SL + 2 : SL + 3]
        return d * e + block[:SL]

    lax.fori_loop(0, NCTX, step, jnp.zeros((SL, HD), F32), unroll=8)


def take_received(received, after):
    return pl.pallas_call(
        take_kernel,
        out_shape=[
            jax.ShapeDtypeStruct((NCTX, KV, HD), BF16),
            jax.ShapeDtypeStruct((NCTX, KV, HD), BF16),
            jax.ShapeDtypeStruct((NCTX, SL, HD), BF16),
        ],
        grid=(1,),
        in_specs=[full(received.shape)] + [TILE] * len(after),
        out_specs=[full((NCTX, KV, HD)), full((NCTX, KV, HD)), full((NCTX, SL, HD))],
        compiler_params=params(),
        cost_estimate=cost(1 << 20, 1 << 21),
    )(received, *after)


def local_kernel(x_ref, b_ref, c_ref, d_ref, o_ref, token_ref):
    token_ref[...] = jnp.zeros((8, HD), F32)
    cum = row_cumulative(d_ref[...])
    cum_col = col_cumulative(d_ref[...])
    cross = lax.dot_general(
        c_ref[...], b_ref[...], (((1,), (1,)), ((), ())), preferred_element_type=F32
    )
    mask = tri(True)
    for h in range(MH):
        gap = jnp.where(mask, cum_col[:, h : h + 1] - cum[h : h + 1, :], -1e30)
        w = (jnp.exp(gap) * cross).astype(BF16)
        o_ref[:, h * HD : (h + 1) * HD] = jnp.dot(
            w, x_ref[:, h * HD : (h + 1) * HD], preferred_element_type=F32
        )


TOKEN = jax.ShapeDtypeStruct((8, HD), F32)


def local_part(x_in, b_in, c_in, decay_log):
    return pl.pallas_call(
        local_kernel,
        out_shape=[jax.ShapeDtypeStruct((L, MH * HD), F32), TOKEN],
        in_specs=[VM] * 4,
        out_specs=[VM] * 2,
        compiler_params=params(LARGE),
        cost_estimate=cost(1 << 28, 1 << 21),
    )(x_in, b_in, c_in, decay_log)


JOIN_COST = 1 << 26


def join_kernel(l_ref, e_ref, c_ref, d_ref, o_ref):
    grow = jnp.exp(col_cumulative(d_ref[...]))
    c = c_ref[...]
    for h in range(MH):
        cols = slice(h * HD, (h + 1) * HD)
        readout = jnp.dot(c, e_ref[cols, :], preferred_element_type=F32)
        o_ref[:, cols] = (l_ref[:, cols] + grow[:, h : h + 1] * readout).astype(BF16)


def join_mamba(local, entering, c_in, decay_log):
    return pl.pallas_call(
        join_kernel,
        out_shape=jax.ShapeDtypeStruct((L, MH * HD), BF16),
        in_specs=[VM] * 4,
        out_specs=VM,
        compiler_params=params(LARGE),
        cost_estimate=cost(JOIN_COST, 1 << 21),
    )(local, entering, c_in, decay_log)


ROWS = QH * L
SCALE2 = LOG2E / math.sqrt(HD)


def stacked_queries(q_ref):
    return jnp.concatenate([q_ref[:, g * HD : (g + 1) * HD] for g in range(QH)], axis=0)


def accumulate(state, s, v):
    m_old, total, acc = state
    m = jnp.maximum(m_old, jnp.max(s, axis=1, keepdims=True))
    factor = jnp.exp2((m_old - m) * SCALE2)
    p = jnp.exp2((s - m) * SCALE2)
    part = p[:, :L]
    for j in range(1, p.shape[1] // L):
        part = part + p[:, j * L : (j + 1) * L]
    added = jnp.dot(p.astype(BF16), v, preferred_element_type=F32)
    return m, total * factor + part, acc * factor + added


def scores(q, k):
    return lax.dot_general(q, k, (((1,), (1,)), ((), ())), preferred_element_type=F32)


def packed(m, total):
    lane = lax.broadcasted_iota(jnp.int32, (ROWS, L), 1)
    return jnp.where(lane < L // 2, m, jnp.sum(total, axis=1, keepdims=True))


def unpacked(ref, at=0):
    lane = lax.broadcasted_iota(jnp.int32, (ROWS, L), 1)
    return ref[:, at : at + 1], jnp.where(lane == 0, ref[:, at + L - 1 : at + L], 0.0)


def open_kernel(q_ref, q2_ref, k_ref, v_ref, _, s_ref, s2_ref, ml_ref, a_ref, token_ref):
    token_ref[...] = jnp.zeros((8, HD), F32)
    q = stacked_queries(q_ref)
    s_ref[...] = q
    s2_ref[...] = stacked_queries(q2_ref)
    s = scores(q, k_ref[...])
    t = lax.broadcasted_iota(jnp.int32, s.shape, 0) % L
    u = lax.broadcasted_iota(jnp.int32, s.shape, 1)
    s = jnp.where(u <= t, s, -1e30)
    m = jnp.max(s, axis=1, keepdims=True)
    p = jnp.exp2((s - m) * SCALE2)
    ml_ref[...] = packed(m, p)
    a_ref[...] = jnp.dot(p.astype(BF16), v_ref[...], preferred_element_type=F32)


PART = jax.ShapeDtypeStruct((ROWS, L), F32)


def open_attention(q_in, q_other, k_in, v_in, after):
    return pl.pallas_call(
        open_kernel,
        out_shape=[jax.ShapeDtypeStruct((ROWS, HD), BF16)] * 2 + [PART] * 2 + [TOKEN],
        in_specs=[VM] * 5,
        out_specs=[VM] * 5,
        compiler_params=params(LARGE),
        cost_estimate=cost(1 << 27, 1 << 20),
    )(q_in, q_other, k_in, v_in, after)


def go_on(me, q, state, sets):
    keys = NCTX * PIECE
    shard = lax.broadcasted_iota(jnp.int32, (1, keys), 1) // PIECE
    bias = jnp.where(shard < me, 0.0, -1e30)
    for ref in sets:
        k = ref[:, 0:PIECE, :].reshape(keys, HD)
        v = ref[:, PIECE:KV, :].reshape(keys, HD)
        state = accumulate(state, scores(q, k) + bias, v)
    return state


def early_kernel(me_ref, q_ref, q2_ref, ml_ref, a_ref, *refs):
    sets, (ml1_ref, a1_ref, ml2_ref, a2_ref) = refs[:2], refs[2:]
    me = me_ref[0]
    m, total, acc = go_on(me, q_ref[...], (*unpacked(ml_ref), a_ref[...]), sets)
    ml1_ref[...] = packed(m, total)
    a1_ref[...] = acc
    none = jnp.full((ROWS, 1), -1e30, F32), jnp.zeros((ROWS, L), F32), jnp.zeros((ROWS, HD), F32)
    m, total, acc = go_on(me ^ 1, q2_ref[...], none, sets)
    ml2_ref[...] = packed(m, total)
    a2_ref[...] = acc


def early_attention(me, q_own, q_other, ml, acc, sets):
    return pl.pallas_call(
        early_kernel,
        out_shape=[PART] * 4,
        in_specs=[SM] + [VM] * 6,
        out_specs=[VM] * 4,
        compiler_params=params(),
        cost_estimate=cost(1 << 29, 1 << 22),
    )(me, q_own, q_other, ml, acc, *sets)


def other_kernel(me_ref, q_ref, ml_ref, a_ref, r_ref, l_ref, o_ref):
    state = (*unpacked(ml_ref), a_ref[...])
    m, total, acc = go_on(me_ref[0] ^ 1, q_ref[...], state, (r_ref, l_ref))
    o_ref[:, :HD] = acc
    o_ref[:, HD:] = packed(m, total)


def own_kernel(me_ref, q_ref, ml_ref, a_ref, r_ref, l_ref, mlo_ref, ao_ref):
    state = (*unpacked(ml_ref), a_ref[...])
    m, total, acc = go_on(me_ref[0], q_ref[...], state, (r_ref, l_ref))
    mlo_ref[...] = packed(m, total)
    ao_ref[...] = acc


def late_attention(kernel, outs, me, queries, ml, acc, sets):
    return pl.pallas_call(
        kernel,
        out_shape=outs,
        in_specs=[SM] + [VM] * 5,
        out_specs=[VM] * len(outs),
        compiler_params=params(),
        cost_estimate=cost(1 << 28, 1 << 21),
    )(me, queries, ml, acc, *sets)


def merge_kernel(ml_ref, a_ref, p_ref, o_ref):
    m1, m2 = ml_ref[:, :1], p_ref[:, HD : HD + 1]
    m = jnp.maximum(m1, m2)
    f1, f2 = jnp.exp2((m1 - m) * SCALE2), jnp.exp2((m2 - m) * SCALE2)
    total = ml_ref[:, L - 1 :] * f1 + p_ref[:, HD + L - 1 :] * f2
    out = (a_ref[...] * f1 + p_ref[:, :HD] * f2) / total
    for g in range(QH):
        o_ref[:, g * HD : (g + 1) * HD] = out[g * L : (g + 1) * L].astype(BF16)


def merge_attention(ml, acc, part):
    return pl.pallas_call(
        merge_kernel,
        out_shape=jax.ShapeDtypeStruct((L, QH * HD), BF16),
        in_specs=[VM] * 3,
        out_specs=VM,
        compiler_params=params(),
        cost_estimate=cost(1 << 20, 1 << 20),
    )(ml, acc, part)


CHIPS_X = 4


def along_x(step):
    pairs = []
    for i in range(NCTX):
        y, x, c = i // (2 * CHIPS_X), i // 2 % CHIPS_X, i % 2
        pairs.append((i, (y * CHIPS_X + (x + step) % CHIPS_X) * 2 + c))
    return pairs


def other_core(value):
    return lax.ppermute(value, "ctx", [(i, i ^ 1) for i in range(NCTX)])


def context_parts(x_in, b_in, c_in, decay_log, q_in, k_in, v_in, expert_out):
    me = lax.axis_index("ctx").astype(jnp.int32).reshape(1)
    chunks = chunks_to_send(x_in, b_in, decay_log, k_in, v_in)
    received = lax.all_to_all(chunks, "ctx", split_axis=0, concat_axis=0, tiled=True)
    q_other = other_core(q_in)
    local, token = local_part(x_in, b_in, c_in, decay_log)
    q_own, q_other, ml, acc, token = open_attention(q_in, q_other, k_in, v_in, token)
    blocks = expert_blocks(expert_out, [chunks.reshape(NCTX * CHUNK, HD), token])
    arrived = sum(b[:8, :HD] for b in blocks[1:]) if len(blocks) > 1 else blocks[0][:8, :HD]
    own, opposite, entering = take_received(received, [arrived])
    right = lax.ppermute(own, "ctx", along_x(1))
    left = lax.ppermute(own, "ctx", along_x(-1))

    ml, acc, ml2, acc2 = early_attention(me, q_own, q_other, ml, acc, [own, opposite])
    entering = lax.all_to_all(entering, "ctx", split_axis=0, concat_axis=0, tiled=True)
    mamba_out = join_mamba(local, entering.reshape(MH * L, HD), c_in, decay_log)

    sets = [right, left]
    both = jax.ShapeDtypeStruct((ROWS, HD + L), F32)
    [part] = late_attention(other_kernel, [both], me, q_other, ml2, acc2, sets)
    part = other_core(part)
    ml, acc = late_attention(own_kernel, [PART] * 2, me, q_own, ml, acc, sets)
    return mamba_out, merge_attention(ml, acc, part), blocks


def blocks_kernel(n_ties, me_ref, e_ref, *refs):
    outs = refs[n_ties:]
    for d, o_ref in enumerate(outs):
        to = lax.rem(me_ref[0] + d, len(outs))
        o_ref[...] = jnp.concatenate(
            [e_ref[0, i, to].astype(F32) for i in range(e_ref.shape[1])], axis=0
        ).astype(BF16)


def combine_kernel(me_ref, idst_ref, gatest_ref, *refs):
    rows_refs, o_ref = refs[:-1], refs[-1]
    peers = len(rows_refs)
    rows = jnp.concatenate([r[...].astype(F32) for r in rows_refs], axis=0).astype(BF16)
    owned = rows.shape[0] // (peers * CAP)
    count = idst_ref.shape[1]
    idst, gatest = idst_ref[...], gatest_ref[...]
    t = lax.broadcasted_iota(jnp.int32, (count, count), 0)
    u = lax.broadcasted_iota(jnp.int32, (count, count), 1)
    place = lax.broadcasted_iota(jnp.int32, (count, rows.shape[0]), 1)

    def column(row):
        return jnp.sum(jnp.where(t == u, row, jnp.zeros_like(row)), axis=1, keepdims=True)

    out = None
    for k in range(2):
        mine = column(idst[k : k + 1, :])
        slot = jnp.zeros((count, 1), jnp.int32)
        for j in range(2):
            before = (u < t) if j >= k else (u <= t)
            same = jnp.logical_and(before, idst[j : j + 1, :] == mine)
            slot = slot + jnp.sum(same.astype(jnp.int32), axis=1, keepdims=True)
        distance = (me_ref[0] - mine // owned + peers) % peers
        number = (distance * owned + mine % owned) * CAP + slot
        pick = (place == number).astype(F32).astype(BF16)
        row = jnp.dot(pick, rows, preferred_element_type=F32)
        term = column(gatest[k : k + 1, :]) * row
        out = term if out is None else out + term
    o_ref[...] = out.astype(BF16)


def expert_blocks(expert_out, after):
    owned, peers, cap, width = expert_out.shape[1:]
    me = lax.axis_index("grp").astype(jnp.int32).reshape(1)
    def kernel(*refs):
        blocks_kernel(len(after), *refs)

    held = pl.pallas_call(
        kernel,
        out_shape=[jax.ShapeDtypeStruct((owned * cap, width), BF16)] * peers,
        grid=(1,),
        in_specs=[SM, full(expert_out.shape)] + [TILE] * len(after),
        out_specs=[full((owned * cap, width))] * peers,
        compiler_params=params(LARGE),
        cost_estimate=cost(1 << 20, 1 << 21),
    )(me, expert_out, *after)
    blocks = list(held)
    for d in sorted(range(1, peers), key=lambda d: (1, 7, 2, 6, 4, 3, 5).index(d)):
        pairs = [(i, (i + d) % peers) for i in range(peers)]
        blocks[d] = lax.ppermute(held[d], "grp", pairs)
    return blocks


def expert_part(expert_ids, gates, blocks):
    me = lax.axis_index("grp").astype(jnp.int32).reshape(1)
    peers = len(blocks)
    rows, width = blocks[0].shape
    count = expert_ids.shape[0]
    return pl.pallas_call(
        combine_kernel,
        grid=(1,),
        out_shape=jax.ShapeDtypeStruct((count, width), BF16),
        in_specs=[SM, full((2, count)), full((2, count))] + [full((rows, width))] * peers,
        out_specs=full((count, width)),
        compiler_params=params(LARGE),
        cost_estimate=cost(1 << 24, 1 << 20),
    )(me, expert_ids.T, gates.T, *blocks)


def shards(x_in, b_in, c_in, decay_log, q_in, k_in, v_in, expert_ids, gates, expert_out):
    mamba_out, attn_out, blocks = context_parts(
        x_in, b_in, c_in, decay_log, q_in, k_in, v_in, expert_out
    )
    moe_out = expert_part(expert_ids, gates, blocks)
    return (mamba_out, attn_out, moe_out)


def solution(mesh):
    return jax.shard_map(
        shards,
        mesh=mesh,
        in_specs=(
            P("ctx", "grp"),
            P("ctx", None),
            P("ctx", None),
            P("grp", "ctx"),
            P("ctx", "grp"),
            P("ctx", "grp"),
            P("ctx", "grp"),
            P(("ctx", "grp"), None),
            P(("ctx", "grp"), None),
            P("ctx", "grp", None, None, None),
        ),
        out_specs=(P("ctx", "grp"), P("ctx", "grp"), P(("ctx", "grp"), None)),
        check_vma=False,
    )
```

```python
import math

import jax
import jax.numpy as jnp
from jax import lax
from jax.experimental import pallas as pl
from jax.experimental.pallas import tpu as pltpu
from jax.sharding import PartitionSpec as P

HD = 128
L = 128
MH = 16
NCTX = 64
QH = 4
CAP = 4
LOG2E = 1.4426950408889634
F32 = jnp.float32
BF16 = jnp.bfloat16
VM = pl.BlockSpec(memory_space=pltpu.VMEM)
SM = pl.BlockSpec(memory_space=pltpu.SMEM)
TILE = pl.BlockSpec((8, 128), lambda i: (0, 0))


LARGE, SMALL = 60, 24


def params(mib=SMALL):
    return pltpu.CompilerParams(vmem_limit_bytes=mib * 2**20)


def full(shape):
    return pl.BlockSpec(shape, lambda i: (0,) * len(shape))


def cost(flops, nbytes):
    return pl.CostEstimate(flops=flops, bytes_accessed=nbytes, transcendentals=0)


def tri(lower):
    r = lax.broadcasted_iota(jnp.int32, (L, L), 0)
    c = lax.broadcasted_iota(jnp.int32, (L, L), 1)
    return (c <= r) if lower else (r <= c)


def row_cumulative(decay):
    return jnp.dot(
        decay, tri(False).astype(F32), precision=lax.Precision.HIGHEST, preferred_element_type=F32
    )


def col_cumulative(decay):
    return lax.dot_general(
        tri(True).astype(F32),
        decay,
        (((1,), (1,)), ((), ())),
        precision=lax.Precision.HIGHEST,
        preferred_element_type=F32,
    )


PIECE = 16
KV = 2 * PIECE
SL = 32
CHUNK = 2 * KV + SL + 8


def send_kernel(x_ref, b_ref, d_ref, k_ref, v_ref, o_ref):
    cum = row_cumulative(d_ref[...])
    tail = jnp.exp(cum[:, L - 1 :] - cum)
    block_decay = jnp.exp(cum[:, L - 1 :])
    bt = b_ref[...].astype(F32).T
    row = lax.broadcasted_iota(jnp.int32, (8, L), 0)
    pieces = L // PIECE
    for h in range(MH):
        wb = (tail[h : h + 1, :] * bt).astype(BF16)
        s = jnp.dot(wb, x_ref[:, h * HD : (h + 1) * HD], preferred_element_type=F32)
        d = jnp.broadcast_to(block_decay[h : h + 1, :], (8, L))
        hi = d.astype(BF16).astype(F32)
        mid = (d - hi).astype(BF16).astype(F32)
        lo = d - hi - mid
        terms = jnp.where(row == 0, hi, jnp.where(row == 1, mid, jnp.where(row == 2, lo, 0.0)))
        for q in range(4):
            j = h * 4 + q
            for turn in range(2):
                at = (j + turn * pieces // 2) % pieces * PIECE
                o_ref[j, turn * KV : turn * KV + PIECE, :] = k_ref[at : at + PIECE, :]
                o_ref[j, turn * KV + PIECE : (turn + 1) * KV, :] = v_ref[at : at + PIECE, :]
            o_ref[j, 2 * KV : CHUNK, :] = jnp.concatenate(
                [s[q * SL : (q + 1) * SL], terms], axis=0
            ).astype(BF16)


def chunks_to_send(x_in, b_in, decay_log, k_in, v_in):
    return pl.pallas_call(
        send_kernel,
        out_shape=jax.ShapeDtypeStruct((NCTX, CHUNK, HD), BF16),
        in_specs=[VM] * 5,
        out_specs=VM,
        compiler_params=params(LARGE),
        cost_estimate=cost(1 << 26, 1 << 21),
    )(x_in, b_in, decay_log, k_in, v_in)


def take_kernel(s_ref, *refs):
    own_ref, opposite_ref, o_ref = refs[-3:]
    own_ref[...] = s_ref[:, :KV, :]
    opposite_ref[...] = s_ref[:, KV : 2 * KV, :]

    def step(k, e):
        o_ref[k] = e.astype(BF16)
        block = s_ref[k, 2 * KV : CHUNK, :].astype(F32)
        d = block[SL : SL + 1] + block[SL + 1 : SL + 2] + block[SL + 2 : SL + 3]
        return d * e + block[:SL]

    lax.fori_loop(0, NCTX, step, jnp.zeros((SL, HD), F32), unroll=8)


def take_received(received, after):
    return pl.pallas_call(
        take_kernel,
        out_shape=[
            jax.ShapeDtypeStruct((NCTX, KV, HD), BF16),
            jax.ShapeDtypeStruct((NCTX, KV, HD), BF16),
            jax.ShapeDtypeStruct((NCTX, SL, HD), BF16),
        ],
        grid=(1,),
        in_specs=[full(received.shape)] + [TILE] * len(after),
        out_specs=[full((NCTX, KV, HD)), full((NCTX, KV, HD)), full((NCTX, SL, HD))],
        compiler_params=params(),
        cost_estimate=cost(1 << 20, 1 << 21),
    )(received, *after)


def local_kernel(x_ref, b_ref, c_ref, d_ref, o_ref, token_ref):
    token_ref[...] = jnp.zeros((8, HD), F32)
    cum = row_cumulative(d_ref[...])
    cum_col = col_cumulative(d_ref[...])
    cross = lax.dot_general(
        c_ref[...], b_ref[...], (((1,), (1,)), ((), ())), preferred_element_type=F32
    )
    mask = tri(True)
    for h in range(MH):
        gap = jnp.where(mask, cum_col[:, h : h + 1] - cum[h : h + 1, :], -1e30)
        w = (jnp.exp(gap) * cross).astype(BF16)
        o_ref[:, h * HD : (h + 1) * HD] = jnp.dot(
            w, x_ref[:, h * HD : (h + 1) * HD], preferred_element_type=F32
        )


TOKEN = jax.ShapeDtypeStruct((8, HD), F32)


def local_part(x_in, b_in, c_in, decay_log):
    return pl.pallas_call(
        local_kernel,
        out_shape=[jax.ShapeDtypeStruct((L, MH * HD), F32), TOKEN],
        in_specs=[VM] * 4,
        out_specs=[VM] * 2,
        compiler_params=params(LARGE),
        cost_estimate=cost(1 << 28, 1 << 21),
    )(x_in, b_in, c_in, decay_log)


JOIN_COST = 1 << 26


def join_kernel(l_ref, e_ref, c_ref, d_ref, _, o_ref):
    grow = jnp.exp(col_cumulative(d_ref[...]))
    c = c_ref[...]
    for h in range(MH):
        cols = slice(h * HD, (h + 1) * HD)
        readout = jnp.dot(c, e_ref[cols, :], preferred_element_type=F32)
        o_ref[:, cols] = (l_ref[:, cols] + grow[:, h : h + 1] * readout).astype(BF16)


def join_mamba(local, entering, c_in, decay_log, after):
    return pl.pallas_call(
        join_kernel,
        grid=(1,),
        out_shape=jax.ShapeDtypeStruct((L, MH * HD), BF16),
        in_specs=[full(a.shape) for a in (local, entering, c_in, decay_log)] + [TILE],
        out_specs=full((L, MH * HD)),
        compiler_params=params(LARGE),
        cost_estimate=cost(JOIN_COST, 1 << 21),
    )(local, entering, c_in, decay_log, after)


ROWS = QH * L
SCALE2 = LOG2E / math.sqrt(HD)


def stacked_queries(q_ref):
    return jnp.concatenate([q_ref[:, g * HD : (g + 1) * HD] for g in range(QH)], axis=0)


def accumulate(state, s, v):
    m_old, total, acc = state
    m = jnp.maximum(m_old, jnp.max(s, axis=1, keepdims=True))
    factor = jnp.exp2((m_old - m) * SCALE2)
    p = jnp.exp2((s - m) * SCALE2)
    part = p[:, :L]
    for j in range(1, p.shape[1] // L):
        part = part + p[:, j * L : (j + 1) * L]
    added = jnp.dot(p.astype(BF16), v, preferred_element_type=F32)
    return m, total * factor + part, acc * factor + added


def scores(q, k):
    return lax.dot_general(q, k, (((1,), (1,)), ((), ())), preferred_element_type=F32)


def packed(m, total):
    lane = lax.broadcasted_iota(jnp.int32, (ROWS, L), 1)
    return jnp.where(lane < L // 2, m, jnp.sum(total, axis=1, keepdims=True))


def unpacked(ref, at=0):
    lane = lax.broadcasted_iota(jnp.int32, (ROWS, L), 1)
    return ref[:, at : at + 1], jnp.where(lane == 0, ref[:, at + L - 1 : at + L], 0.0)


def open_kernel(q_ref, q2_ref, k_ref, v_ref, _, s_ref, s2_ref, ml_ref, a_ref, token_ref):
    token_ref[...] = jnp.zeros((8, HD), F32)
    q = stacked_queries(q_ref)
    s_ref[...] = q
    s2_ref[...] = stacked_queries(q2_ref)
    s = scores(q, k_ref[...])
    t = lax.broadcasted_iota(jnp.int32, s.shape, 0) % L
    u = lax.broadcasted_iota(jnp.int32, s.shape, 1)
    s = jnp.where(u <= t, s, -1e30)
    m = jnp.max(s, axis=1, keepdims=True)
    p = jnp.exp2((s - m) * SCALE2)
    ml_ref[...] = packed(m, p)
    a_ref[...] = jnp.dot(p.astype(BF16), v_ref[...], preferred_element_type=F32)


PART = jax.ShapeDtypeStruct((ROWS, L), F32)


def open_attention(q_in, q_other, k_in, v_in, after):
    return pl.pallas_call(
        open_kernel,
        out_shape=[jax.ShapeDtypeStruct((ROWS, HD), BF16)] * 2 + [PART] * 2 + [TOKEN],
        in_specs=[VM] * 5,
        out_specs=[VM] * 5,
        compiler_params=params(LARGE),
        cost_estimate=cost(1 << 27, 1 << 20),
    )(q_in, q_other, k_in, v_in, after)


def go_on(me, q, state, sets):
    keys = NCTX * PIECE
    shard = lax.broadcasted_iota(jnp.int32, (1, keys), 1) // PIECE
    bias = jnp.where(shard < me, 0.0, -1e30)
    for ref in sets:
        k = ref[:, 0:PIECE, :].reshape(keys, HD)
        v = ref[:, PIECE:KV, :].reshape(keys, HD)
        state = accumulate(state, scores(q, k) + bias, v)
    return state


def early_kernel(me_ref, q_ref, q2_ref, ml_ref, a_ref, *refs):
    sets, (ml1_ref, a1_ref, ml2_ref, a2_ref) = refs[:2], refs[2:]
    me = me_ref[0]
    m, total, acc = go_on(me, q_ref[...], (*unpacked(ml_ref), a_ref[...]), sets)
    ml1_ref[...] = packed(m, total)
    a1_ref[...] = acc
    none = jnp.full((ROWS, 1), -1e30, F32), jnp.zeros((ROWS, L), F32), jnp.zeros((ROWS, HD), F32)
    m, total, acc = go_on(me ^ 1, q2_ref[...], none, sets)
    ml2_ref[...] = packed(m, total)
    a2_ref[...] = acc


def early_attention(me, q_own, q_other, ml, acc, sets):
    return pl.pallas_call(
        early_kernel,
        out_shape=[PART] * 4,
        in_specs=[SM] + [VM] * 6,
        out_specs=[VM] * 4,
        compiler_params=params(),
        cost_estimate=cost(1 << 29, 1 << 22),
    )(me, q_own, q_other, ml, acc, *sets)


def other_kernel(me_ref, q_ref, ml_ref, a_ref, r_ref, l_ref, o_ref):
    state = (*unpacked(ml_ref), a_ref[...])
    m, total, acc = go_on(me_ref[0] ^ 1, q_ref[...], state, (r_ref, l_ref))
    o_ref[:, :HD] = acc
    o_ref[:, HD:] = packed(m, total)


def own_kernel(me_ref, q_ref, ml_ref, a_ref, r_ref, l_ref, mlo_ref, ao_ref):
    state = (*unpacked(ml_ref), a_ref[...])
    m, total, acc = go_on(me_ref[0], q_ref[...], state, (r_ref, l_ref))
    mlo_ref[...] = packed(m, total)
    ao_ref[...] = acc


def late_attention(kernel, outs, me, queries, ml, acc, sets):
    return pl.pallas_call(
        kernel,
        out_shape=outs,
        in_specs=[SM] + [VM] * 5,
        out_specs=[VM] * len(outs),
        compiler_params=params(),
        cost_estimate=cost(1 << 28, 1 << 21),
    )(me, queries, ml, acc, *sets)


def merge_kernel(ml_ref, a_ref, p_ref, o_ref):
    m1, m2 = ml_ref[:, :1], p_ref[:, HD : HD + 1]
    m = jnp.maximum(m1, m2)
    f1, f2 = jnp.exp2((m1 - m) * SCALE2), jnp.exp2((m2 - m) * SCALE2)
    total = ml_ref[:, L - 1 :] * f1 + p_ref[:, HD + L - 1 :] * f2
    out = (a_ref[...] * f1 + p_ref[:, :HD] * f2) / total
    for g in range(QH):
        o_ref[:, g * HD : (g + 1) * HD] = out[g * L : (g + 1) * L].astype(BF16)


def merge_attention(ml, acc, part):
    return pl.pallas_call(
        merge_kernel,
        out_shape=jax.ShapeDtypeStruct((L, QH * HD), BF16),
        in_specs=[VM] * 3,
        out_specs=VM,
        compiler_params=params(),
        cost_estimate=cost(1 << 20, 1 << 20),
    )(ml, acc, part)


CHIPS_X = 4


def along_x(step):
    pairs = []
    for i in range(NCTX):
        y, x, c = i // (2 * CHIPS_X), i // 2 % CHIPS_X, i % 2
        pairs.append((i, (y * CHIPS_X + (x + step) % CHIPS_X) * 2 + c))
    return pairs


def other_core(value):
    return lax.ppermute(value, "ctx", [(i, i ^ 1) for i in range(NCTX)])


def context_parts(x_in, b_in, c_in, decay_log, q_in, k_in, v_in, expert_out):
    me = lax.axis_index("ctx").astype(jnp.int32).reshape(1)
    chunks = chunks_to_send(x_in, b_in, decay_log, k_in, v_in)
    received = lax.all_to_all(chunks, "ctx", split_axis=0, concat_axis=0, tiled=True)
    q_other = other_core(q_in)
    local, token = local_part(x_in, b_in, c_in, decay_log)
    q_own, q_other, ml, acc, token = open_attention(q_in, q_other, k_in, v_in, token)
    blocks = expert_blocks(expert_out, [chunks.reshape(NCTX * CHUNK, HD)])
    arrived = sum((b[:8, :HD] for b in blocks[1:]), token.astype(BF16))
    own, opposite, entering = take_received(received, [arrived])
    right = lax.ppermute(own, "ctx", along_x(1))
    left = lax.ppermute(own, "ctx", along_x(-1))

    ml, acc, ml2, acc2 = early_attention(me, q_own, q_other, ml, acc, [own, opposite])
    entering = lax.all_to_all(entering, "ctx", split_axis=0, concat_axis=0, tiled=True)

    sets = [right, left]
    both = jax.ShapeDtypeStruct((ROWS, HD + L), F32)
    [part] = late_attention(other_kernel, [both], me, q_other, ml2, acc2, sets)
    part = other_core(part)
    ml, acc = late_attention(own_kernel, [PART] * 2, me, q_own, ml, acc, sets)
    attn_out = merge_attention(ml, acc, part)
    mamba_out = join_mamba(local, entering.reshape(MH * L, HD), c_in, decay_log, attn_out)
    return mamba_out, attn_out, blocks


def blocks_kernel(n_ties, me_ref, e_ref, *refs):
    outs = refs[n_ties:]
    for d, o_ref in enumerate(outs):
        to = lax.rem(me_ref[0] + d, len(outs))
        o_ref[...] = jnp.concatenate(
            [e_ref[0, i, to].astype(F32) for i in range(e_ref.shape[1])], axis=0
        ).astype(BF16)


def combine_kernel(me_ref, idst_ref, gatest_ref, *refs):
    rows_refs, o_ref = refs[:-1], refs[-1]
    peers = len(rows_refs)
    rows = jnp.concatenate([r[...].astype(F32) for r in rows_refs], axis=0).astype(BF16)
    owned = rows.shape[0] // (peers * CAP)
    count = idst_ref.shape[1]
    idst, gatest = idst_ref[...], gatest_ref[...]
    t = lax.broadcasted_iota(jnp.int32, (count, count), 0)
    u = lax.broadcasted_iota(jnp.int32, (count, count), 1)
    place = lax.broadcasted_iota(jnp.int32, (count, rows.shape[0]), 1)

    def column(row):
        return jnp.sum(jnp.where(t == u, row, jnp.zeros_like(row)), axis=1, keepdims=True)

    out = None
    for k in range(2):
        mine = column(idst[k : k + 1, :])
        slot = jnp.zeros((count, 1), jnp.int32)
        for j in range(2):
            before = (u < t) if j >= k else (u <= t)
            same = jnp.logical_and(before, idst[j : j + 1, :] == mine)
            slot = slot + jnp.sum(same.astype(jnp.int32), axis=1, keepdims=True)
        distance = (me_ref[0] - mine // owned + peers) % peers
        number = (distance * owned + mine % owned) * CAP + slot
        pick = (place == number).astype(F32).astype(BF16)
        row = jnp.dot(pick, rows, preferred_element_type=F32)
        term = column(gatest[k : k + 1, :]) * row
        out = term if out is None else out + term
    o_ref[...] = out.astype(BF16)


def expert_blocks(expert_out, after):
    owned, peers, cap, width = expert_out.shape[1:]
    me = lax.axis_index("grp").astype(jnp.int32).reshape(1)
    def kernel(*refs):
        blocks_kernel(len(after), *refs)

    held = pl.pallas_call(
        kernel,
        out_shape=[jax.ShapeDtypeStruct((owned * cap, width), BF16)] * peers,
        grid=(1,),
        in_specs=[SM, full(expert_out.shape)] + [TILE] * len(after),
        out_specs=[full((owned * cap, width))] * peers,
        compiler_params=params(LARGE),
        cost_estimate=cost(1 << 20, 1 << 21),
    )(me, expert_out, *after)
    blocks = list(held)
    for d in sorted(range(1, peers), key=lambda d: (1, 7, 2, 6, 4, 3, 5).index(d)):
        pairs = [(i, (i + d) % peers) for i in range(peers)]
        blocks[d] = lax.ppermute(held[d], "grp", pairs)
    return blocks


def expert_part(expert_ids, gates, blocks):
    me = lax.axis_index("grp").astype(jnp.int32).reshape(1)
    peers = len(blocks)
    rows, width = blocks[0].shape
    count = expert_ids.shape[0]
    return pl.pallas_call(
        combine_kernel,
        grid=(1,),
        out_shape=jax.ShapeDtypeStruct((count, width), BF16),
        in_specs=[SM, full((2, count)), full((2, count))] + [full((rows, width))] * peers,
        out_specs=full((count, width)),
        compiler_params=params(LARGE),
        cost_estimate=cost(1 << 24, 1 << 20),
    )(me, expert_ids.T, gates.T, *blocks)


def shards(x_in, b_in, c_in, decay_log, q_in, k_in, v_in, expert_ids, gates, expert_out):
    mamba_out, attn_out, blocks = context_parts(
        x_in, b_in, c_in, decay_log, q_in, k_in, v_in, expert_out
    )
    moe_out = expert_part(expert_ids, gates, blocks)
    return (mamba_out, attn_out, moe_out)


def solution(mesh):
    return jax.shard_map(
        shards,
        mesh=mesh,
        in_specs=(
            P("ctx", "grp"),
            P("ctx", None),
            P("ctx", None),
            P("grp", "ctx"),
            P("ctx", "grp"),
            P("ctx", "grp"),
            P("ctx", "grp"),
            P(("ctx", "grp"), None),
            P(("ctx", "grp"), None),
            P("ctx", "grp", None, None, None),
        ),
        out_specs=(P("ctx", "grp"), P("ctx", "grp"), P(("ctx", "grp"), None)),
        check_vma=False,
    )
```

```python
import math

import jax
import jax.numpy as jnp
from jax import lax
from jax.experimental import pallas as pl
from jax.experimental.pallas import tpu as pltpu
from jax.sharding import PartitionSpec as P

HD = 128
L = 128
MH = 16
NCTX = 64
QH = 4
CAP = 4
LOG2E = 1.4426950408889634
F32 = jnp.float32
BF16 = jnp.bfloat16
VM = pl.BlockSpec(memory_space=pltpu.VMEM)
SM = pl.BlockSpec(memory_space=pltpu.SMEM)
TILE = pl.BlockSpec((8, 128), lambda i: (0, 0))


LARGE, SMALL = 60, 24


def params(mib=SMALL):
    return pltpu.CompilerParams(vmem_limit_bytes=mib * 2**20)


def full(shape):
    return pl.BlockSpec(shape, lambda i: (0,) * len(shape))


def cost(flops, nbytes):
    return pl.CostEstimate(flops=flops, bytes_accessed=nbytes, transcendentals=0)


def tri(lower):
    r = lax.broadcasted_iota(jnp.int32, (L, L), 0)
    c = lax.broadcasted_iota(jnp.int32, (L, L), 1)
    return (c <= r) if lower else (r <= c)


def row_cumulative(decay):
    return jnp.dot(
        decay, tri(False).astype(F32), precision=lax.Precision.HIGHEST, preferred_element_type=F32
    )


def col_cumulative(decay):
    return lax.dot_general(
        tri(True).astype(F32),
        decay,
        (((1,), (1,)), ((), ())),
        precision=lax.Precision.HIGHEST,
        preferred_element_type=F32,
    )


PIECE = 16
KV = 2 * PIECE
SL = 32
CHUNK = 2 * KV + SL + 8


def send_kernel(x_ref, b_ref, d_ref, k_ref, v_ref, o_ref):
    cum = row_cumulative(d_ref[...])
    tail = jnp.exp(cum[:, L - 1 :] - cum)
    block_decay = jnp.exp(cum[:, L - 1 :])
    bt = b_ref[...].astype(F32).T
    row = lax.broadcasted_iota(jnp.int32, (8, L), 0)
    pieces = L // PIECE
    for h in range(MH):
        wb = (tail[h : h + 1, :] * bt).astype(BF16)
        s = jnp.dot(wb, x_ref[:, h * HD : (h + 1) * HD], preferred_element_type=F32)
        d = jnp.broadcast_to(block_decay[h : h + 1, :], (8, L))
        hi = d.astype(BF16).astype(F32)
        mid = (d - hi).astype(BF16).astype(F32)
        lo = d - hi - mid
        terms = jnp.where(row == 0, hi, jnp.where(row == 1, mid, jnp.where(row == 2, lo, 0.0)))
        for q in range(4):
            j = h * 4 + q
            for turn in range(2):
                at = (j + turn * pieces // 2) % pieces * PIECE
                o_ref[j, turn * KV : turn * KV + PIECE, :] = k_ref[at : at + PIECE, :]
                o_ref[j, turn * KV + PIECE : (turn + 1) * KV, :] = v_ref[at : at + PIECE, :]
            o_ref[j, 2 * KV : CHUNK, :] = jnp.concatenate(
                [s[q * SL : (q + 1) * SL], terms], axis=0
            ).astype(BF16)


def chunks_to_send(x_in, b_in, decay_log, k_in, v_in):
    return pl.pallas_call(
        send_kernel,
        out_shape=jax.ShapeDtypeStruct((NCTX, CHUNK, HD), BF16),
        in_specs=[VM] * 5,
        out_specs=VM,
        compiler_params=params(LARGE),
        cost_estimate=cost(1 << 26, 1 << 21),
    )(x_in, b_in, decay_log, k_in, v_in)


def take_kernel(s_ref, *refs):
    own_ref, opposite_ref, o_ref = refs[-3:]
    own_ref[...] = s_ref[:, :KV, :]
    opposite_ref[...] = s_ref[:, KV : 2 * KV, :]

    def step(k, e):
        o_ref[k] = e.astype(BF16)
        block = s_ref[k, 2 * KV : CHUNK, :].astype(F32)
        d = block[SL : SL + 1] + block[SL + 1 : SL + 2] + block[SL + 2 : SL + 3]
        return d * e + block[:SL]

    lax.fori_loop(0, NCTX, step, jnp.zeros((SL, HD), F32), unroll=8)


def take_received(received, after):
    return pl.pallas_call(
        take_kernel,
        out_shape=[
            jax.ShapeDtypeStruct((NCTX, KV, HD), BF16),
            jax.ShapeDtypeStruct((NCTX, KV, HD), BF16),
            jax.ShapeDtypeStruct((NCTX, SL, HD), BF16),
        ],
        grid=(1,),
        in_specs=[full(received.shape)] + [TILE] * len(after),
        out_specs=[full((NCTX, KV, HD)), full((NCTX, KV, HD)), full((NCTX, SL, HD))],
        compiler_params=params(),
        cost_estimate=cost(1 << 20, 1 << 21),
    )(received, *after)


def local_kernel(x_ref, b_ref, c_ref, d_ref, o_ref, grow_ref, token_ref):
    token_ref[...] = jnp.zeros((8, HD), F32)
    cum = row_cumulative(d_ref[...])
    cum_col = col_cumulative(d_ref[...])
    grow_ref[...] = jnp.exp(cum_col)
    cross = lax.dot_general(
        c_ref[...], b_ref[...], (((1,), (1,)), ((), ())), preferred_element_type=F32
    )
    mask = tri(True)
    for h in range(MH):
        gap = jnp.where(mask, cum_col[:, h : h + 1] - cum[h : h + 1, :], -1e30)
        w = (jnp.exp(gap) * cross).astype(BF16)
        o_ref[:, h * HD : (h + 1) * HD] = jnp.dot(
            w, x_ref[:, h * HD : (h + 1) * HD], preferred_element_type=F32
        )


TOKEN = jax.ShapeDtypeStruct((8, HD), F32)


def local_part(x_in, b_in, c_in, decay_log):
    return pl.pallas_call(
        local_kernel,
        out_shape=[
            jax.ShapeDtypeStruct((L, MH * HD), F32),
            jax.ShapeDtypeStruct((L, MH), F32),
            TOKEN,
        ],
        in_specs=[VM] * 4,
        out_specs=[VM] * 3,
        compiler_params=params(LARGE),
        cost_estimate=cost(1 << 28, 1 << 21),
    )(x_in, b_in, c_in, decay_log)


JOIN_COST = 1 << 26


def join_kernel(l_ref, e_ref, c_ref, g_ref, _, o_ref):
    grow = g_ref[...]
    c = c_ref[...]
    for h in range(MH):
        cols = slice(h * HD, (h + 1) * HD)
        readout = jnp.dot(c, e_ref[cols, :], preferred_element_type=F32)
        o_ref[:, cols] = (l_ref[:, cols] + grow[:, h : h + 1] * readout).astype(BF16)


def join_mamba(local, entering, c_in, grow, after):
    return pl.pallas_call(
        join_kernel,
        grid=(1,),
        out_shape=jax.ShapeDtypeStruct((L, MH * HD), BF16),
        in_specs=[full(a.shape) for a in (local, entering, c_in, grow)] + [TILE],
        out_specs=full((L, MH * HD)),
        compiler_params=params(LARGE),
        cost_estimate=cost(JOIN_COST, 1 << 21),
    )(local, entering, c_in, grow, after)


ROWS = QH * L
SCALE2 = LOG2E / math.sqrt(HD)


def stacked_queries(q_ref):
    return jnp.concatenate([q_ref[:, g * HD : (g + 1) * HD] for g in range(QH)], axis=0)


def accumulate(state, s, v):
    m_old, total, acc = state
    m = jnp.maximum(m_old, jnp.max(s, axis=1, keepdims=True))
    factor = jnp.exp2((m_old - m) * SCALE2)
    p = jnp.exp2((s - m) * SCALE2)
    part = p[:, :L]
    for j in range(1, p.shape[1] // L):
        part = part + p[:, j * L : (j + 1) * L]
    added = jnp.dot(p.astype(BF16), v, preferred_element_type=F32)
    return m, total * factor + part, acc * factor + added


def scores(q, k):
    return lax.dot_general(q, k, (((1,), (1,)), ((), ())), preferred_element_type=F32)


def packed(m, total):
    lane = lax.broadcasted_iota(jnp.int32, (ROWS, L), 1)
    return jnp.where(lane < L // 2, m, jnp.sum(total, axis=1, keepdims=True))


def unpacked(ref, at=0):
    lane = lax.broadcasted_iota(jnp.int32, (ROWS, L), 1)
    return ref[:, at : at + 1], jnp.where(lane == 0, ref[:, at + L - 1 : at + L], 0.0)


def stack_kernel(q_ref, q2_ref, _, s_ref, s2_ref, token_ref):
    token_ref[...] = jnp.zeros((8, HD), F32)
    s_ref[...] = stacked_queries(q_ref)
    s2_ref[...] = stacked_queries(q2_ref)


PART = jax.ShapeDtypeStruct((ROWS, L), F32)


def stack_both(q_in, q_other, after):
    return pl.pallas_call(
        stack_kernel,
        out_shape=[jax.ShapeDtypeStruct((ROWS, HD), BF16)] * 2 + [TOKEN],
        in_specs=[VM] * 3,
        out_specs=[VM] * 3,
        compiler_params=params(LARGE),
        cost_estimate=cost(1 << 20, 1 << 19),
    )(q_in, q_other, after)


def go_on(me, q, state, sets):
    keys = NCTX * PIECE
    shard = lax.broadcasted_iota(jnp.int32, (1, keys), 1) // PIECE
    bias = jnp.where(shard < me, 0.0, -1e30)
    for ref in sets:
        k = ref[:, 0:PIECE, :].reshape(keys, HD)
        v = ref[:, PIECE:KV, :].reshape(keys, HD)
        state = accumulate(state, scores(q, k) + bias, v)
    return state


def early_kernel(me_ref, q_ref, q2_ref, k_ref, v_ref, *refs):
    sets, (ml1_ref, a1_ref, ml2_ref, a2_ref) = refs[:2], refs[2:]
    me = me_ref[0]
    q = q_ref[...]
    s = scores(q, k_ref[...])
    t = lax.broadcasted_iota(jnp.int32, s.shape, 0) % L
    u = lax.broadcasted_iota(jnp.int32, s.shape, 1)
    s = jnp.where(u <= t, s, -1e30)
    m = jnp.max(s, axis=1, keepdims=True)
    p = jnp.exp2((s - m) * SCALE2)
    acc = jnp.dot(p.astype(BF16), v_ref[...], preferred_element_type=F32)
    m, total, acc = go_on(me, q, (m, p, acc), sets)
    ml1_ref[...] = packed(m, total)
    a1_ref[...] = acc
    none = jnp.full((ROWS, 1), -1e30, F32), jnp.zeros((ROWS, L), F32), jnp.zeros((ROWS, HD), F32)
    m, total, acc = go_on(me ^ 1, q2_ref[...], none, sets)
    ml2_ref[...] = packed(m, total)
    a2_ref[...] = acc


def early_attention(me, q_own, q_other, k_in, v_in, sets):
    return pl.pallas_call(
        early_kernel,
        out_shape=[PART] * 4,
        in_specs=[SM] + [VM] * 6,
        out_specs=[VM] * 4,
        compiler_params=params(),
        cost_estimate=cost(1 << 29, 1 << 22),
    )(me, q_own, q_other, k_in, v_in, *sets)


def other_kernel(me_ref, q_ref, ml_ref, a_ref, r_ref, l_ref, o_ref):
    state = (*unpacked(ml_ref), a_ref[...])
    m, total, acc = go_on(me_ref[0] ^ 1, q_ref[...], state, (r_ref, l_ref))
    o_ref[:, :HD] = acc
    o_ref[:, HD:] = packed(m, total)


def own_kernel(me_ref, q_ref, ml_ref, a_ref, r_ref, l_ref, mlo_ref, ao_ref):
    state = (*unpacked(ml_ref), a_ref[...])
    m, total, acc = go_on(me_ref[0], q_ref[...], state, (r_ref, l_ref))
    mlo_ref[...] = packed(m, total)
    ao_ref[...] = acc


def late_attention(kernel, outs, me, queries, ml, acc, sets):
    return pl.pallas_call(
        kernel,
        out_shape=outs,
        in_specs=[SM] + [VM] * 5,
        out_specs=[VM] * len(outs),
        compiler_params=params(),
        cost_estimate=cost(1 << 28, 1 << 21),
    )(me, queries, ml, acc, *sets)


def merge_kernel(ml_ref, a_ref, p_ref, o_ref):
    m1, m2 = ml_ref[:, :1], p_ref[:, HD : HD + 1]
    m = jnp.maximum(m1, m2)
    f1, f2 = jnp.exp2((m1 - m) * SCALE2), jnp.exp2((m2 - m) * SCALE2)
    total = ml_ref[:, L - 1 :] * f1 + p_ref[:, HD + L - 1 :] * f2
    out = (a_ref[...] * f1 + p_ref[:, :HD] * f2) / total
    for g in range(QH):
        o_ref[:, g * HD : (g + 1) * HD] = out[g * L : (g + 1) * L].astype(BF16)


def merge_attention(ml, acc, part):
    return pl.pallas_call(
        merge_kernel,
        out_shape=jax.ShapeDtypeStruct((L, QH * HD), BF16),
        in_specs=[VM] * 3,
        out_specs=VM,
        compiler_params=params(),
        cost_estimate=cost(1 << 20, 1 << 20),
    )(ml, acc, part)


CHIPS_X = 4


def along_x(step):
    pairs = []
    for i in range(NCTX):
        y, x, c = i // (2 * CHIPS_X), i // 2 % CHIPS_X, i % 2
        pairs.append((i, (y * CHIPS_X + (x + step) % CHIPS_X) * 2 + c))
    return pairs


def other_core(value):
    return lax.ppermute(value, "ctx", [(i, i ^ 1) for i in range(NCTX)])


def context_parts(x_in, b_in, c_in, decay_log, q_in, k_in, v_in, expert_out):
    me = lax.axis_index("ctx").astype(jnp.int32).reshape(1)
    chunks = chunks_to_send(x_in, b_in, decay_log, k_in, v_in)
    received = lax.all_to_all(chunks, "ctx", split_axis=0, concat_axis=0, tiled=True)
    q_other = other_core(q_in)
    local, grow, token = local_part(x_in, b_in, c_in, decay_log)
    q_own, q_other, token = stack_both(q_in, q_other, token)
    blocks = expert_blocks(expert_out, [chunks.reshape(NCTX * CHUNK, HD)])
    arrived = sum((b[:8, :HD] for b in blocks[1:]), token.astype(BF16))
    own, opposite, entering = take_received(received, [arrived])
    right = lax.ppermute(own, "ctx", along_x(1))
    left = lax.ppermute(own, "ctx", along_x(-1))

    ml, acc, ml2, acc2 = early_attention(me, q_own, q_other, k_in, v_in, [own, opposite])
    entering = lax.all_to_all(entering, "ctx", split_axis=0, concat_axis=0, tiled=True)

    sets = [right, left]
    both = jax.ShapeDtypeStruct((ROWS, HD + L), F32)
    [part] = late_attention(other_kernel, [both], me, q_other, ml2, acc2, sets)
    part = other_core(part)
    ml, acc = late_attention(own_kernel, [PART] * 2, me, q_own, ml, acc, sets)
    attn_out = merge_attention(ml, acc, part)
    mamba_out = join_mamba(local, entering.reshape(MH * L, HD), c_in, grow, attn_out)
    return mamba_out, attn_out, blocks


def blocks_kernel(n_ties, me_ref, e_ref, *refs):
    outs = refs[n_ties:]
    for d, o_ref in enumerate(outs):
        to = lax.rem(me_ref[0] + d, len(outs))
        o_ref[...] = jnp.concatenate(
            [e_ref[0, i, to].astype(F32) for i in range(e_ref.shape[1])], axis=0
        ).astype(BF16)


def combine_kernel(me_ref, idst_ref, gatest_ref, *refs):
    rows_refs, o_ref = refs[:-1], refs[-1]
    peers = len(rows_refs)
    rows = jnp.concatenate([r[...].astype(F32) for r in rows_refs], axis=0).astype(BF16)
    owned = rows.shape[0] // (peers * CAP)
    count = idst_ref.shape[1]
    idst, gatest = idst_ref[...], gatest_ref[...]
    t = lax.broadcasted_iota(jnp.int32, (count, count), 0)
    u = lax.broadcasted_iota(jnp.int32, (count, count), 1)
    place = lax.broadcasted_iota(jnp.int32, (count, rows.shape[0]), 1)

    def column(row):
        return jnp.sum(jnp.where(t == u, row, jnp.zeros_like(row)), axis=1, keepdims=True)

    out = None
    for k in range(2):
        mine = column(idst[k : k + 1, :])
        slot = jnp.zeros((count, 1), jnp.int32)
        for j in range(2):
            before = (u < t) if j >= k else (u <= t)
            same = jnp.logical_and(before, idst[j : j + 1, :] == mine)
            slot = slot + jnp.sum(same.astype(jnp.int32), axis=1, keepdims=True)
        distance = (me_ref[0] - mine // owned + peers) % peers
        number = (distance * owned + mine % owned) * CAP + slot
        pick = (place == number).astype(F32).astype(BF16)
        row = jnp.dot(pick, rows, preferred_element_type=F32)
        term = column(gatest[k : k + 1, :]) * row
        out = term if out is None else out + term
    o_ref[...] = out.astype(BF16)


def expert_blocks(expert_out, after):
    owned, peers, cap, width = expert_out.shape[1:]
    me = lax.axis_index("grp").astype(jnp.int32).reshape(1)
    def kernel(*refs):
        blocks_kernel(len(after), *refs)

    held = pl.pallas_call(
        kernel,
        out_shape=[jax.ShapeDtypeStruct((owned * cap, width), BF16)] * peers,
        grid=(1,),
        in_specs=[SM, full(expert_out.shape)] + [TILE] * len(after),
        out_specs=[full((owned * cap, width))] * peers,
        compiler_params=params(LARGE),
        cost_estimate=cost(1 << 20, 1 << 21),
    )(me, expert_out, *after)
    blocks = list(held)
    for d in sorted(range(1, peers), key=lambda d: (1, 7, 2, 6, 4, 3, 5).index(d)):
        pairs = [(i, (i + d) % peers) for i in range(peers)]
        blocks[d] = lax.ppermute(held[d], "grp", pairs)
    return blocks


def expert_part(expert_ids, gates, blocks):
    me = lax.axis_index("grp").astype(jnp.int32).reshape(1)
    peers = len(blocks)
    rows, width = blocks[0].shape
    count = expert_ids.shape[0]
    return pl.pallas_call(
        combine_kernel,
        grid=(1,),
        out_shape=jax.ShapeDtypeStruct((count, width), BF16),
        in_specs=[SM, full((2, count)), full((2, count))] + [full((rows, width))] * peers,
        out_specs=full((count, width)),
        compiler_params=params(LARGE),
        cost_estimate=cost(1 << 24, 1 << 20),
    )(me, expert_ids.T, gates.T, *blocks)


def shards(x_in, b_in, c_in, decay_log, q_in, k_in, v_in, expert_ids, gates, expert_out):
    mamba_out, attn_out, blocks = context_parts(
        x_in, b_in, c_in, decay_log, q_in, k_in, v_in, expert_out
    )
    moe_out = expert_part(expert_ids, gates, blocks)
    return (mamba_out, attn_out, moe_out)


def solution(mesh):
    return jax.shard_map(
        shards,
        mesh=mesh,
        in_specs=(
            P("ctx", "grp"),
            P("ctx", None),
            P("ctx", None),
            P("grp", "ctx"),
            P("ctx", "grp"),
            P("ctx", "grp"),
            P("ctx", "grp"),
            P(("ctx", "grp"), None),
            P(("ctx", "grp"), None),
            P("ctx", "grp", None, None, None),
        ),
        out_specs=(P("ctx", "grp"), P("ctx", "grp"), P(("ctx", "grp"), None)),
        check_vma=False,
    )
```
